512 devices in a mesh: tm: 128 (over y, z, core), row: 2 (over x_hi), col: 2 (over x_lo).
Axes of the slice: x: 4 (x_hi: 2, x_lo: 2; x = x_hi * 2 + x_lo), y: 8, z: 8, core: 2. Of those that a mesh axis runs over, the one named last changes fastest.
Arguments:
- observed: float32 [8192, 16, 256], P('tm', 'row', 'col'), may hold values from -6 to 6
- kernel: float32 [33, 16, 256], P(None, 'row', 'col'), may hold values from 0.05 to 1
Outputs:
- restored: float32 [8192, 16, 256], P('tm', 'row', 'col')
The draws below stay inside these ranges and needn't reach their ends.
All inputs are finite; a program needn't handle non-finite values.
Results may differ from the reference program's by a relative error of at most 0.00002.
Values sent between devices are 32-bit elements; how exact they have to be, the bound alone decides.
No kernel may reach another device: no remote copies, remote signals or barrier semaphores. Data moves between devices by JAX's collectives and lax.ppermute only.
A program may use at most 128 MiB of HBM per device.

```python
import math
import jax
import jax.numpy as jnp
from jax import lax

TAPS = 33
ITERS = 1
PASSES = 2
FRAMES = 8192
HEIGHT = 16
WIDTH = 256


def block_levels(stream_key, shape, cuts, least, largest):
    loudness, own = 1.0, jax.random.fold_in(stream_key, 6)
    for position, parts in cuts:
        steps = jnp.exp(jax.random.uniform(jax.random.fold_in(own, position), (parts,), jnp.float32, least / len(cuts), largest / len(cuts)))
        loudness = loudness * jnp.repeat(steps, shape[position] // parts).reshape([-1 if axis == position else 1 for axis in range(len(shape))])
    return loudness


def noise(stream_key, extent, spread, limit, cuts=(), held_as=jnp.bfloat16):
    array = jax.random.normal(stream_key, extent, jnp.float32) * spread
    if len(cuts) > 0:
        array = block_levels(stream_key, extent, cuts, -0.22, 0.18) * array
    return jnp.clip(array, min=-limit, max=limit).astype(held_as)


def setup_inputs(seed: int = 0) -> dict:
    streams_of = jax.random.split(jax.random.key(seed), 3)
    observed = noise(streams_of[0], (FRAMES, HEIGHT, WIDTH), 1.0, 6.0, ((0, 128), (1, 2), (2, 2)), jnp.float32)
    kernel = jnp.clip(jnp.exp(math.log(1.0) - 2.9957323 * jax.random.uniform(streams_of[1], (TAPS, HEIGHT, WIDTH), jnp.float32) ** block_levels(streams_of[1], (TAPS, HEIGHT, WIDTH), ((1, 2), (2, 2)), -0.2, 0.2)), 0.05, 1.0)
    return dict(observed=observed, kernel=kernel)


primal_step = 1.0
dual_step = 0.5
tv_weight = 0.1
inner_step = 1.0 / 12.0

def blur_forward(field, kern):
    half = (TAPS - 1) // 2
    frames = field.shape[0]
    padded = jnp.pad(field, ((half, half), (0, 0), (0, 0)))
    result = jnp.zeros_like(field)
    for tap in range(TAPS):
        result = result + kern[tap] * padded[tap:tap + frames]
    return result

def blur_adjoint(field, kern):
    half = (TAPS - 1) // 2
    frames = field.shape[0]
    padded = jnp.pad(field, ((half, half), (0, 0), (0, 0)))
    result = jnp.zeros_like(field)
    for tap in range(TAPS):
        result = result + kern[tap] * padded[2 * half - tap:2 * half - tap + frames]
    return result

def gradient(field):
    zero_t = jnp.zeros_like(field[:1])
    grad_t = jnp.concatenate([field[1:] - field[:-1], zero_t], axis=0)
    zero_r = jnp.zeros_like(field[:, :1])
    grad_r = jnp.concatenate([field[:, 1:] - field[:, :-1], zero_r], axis=1)
    zero_c = jnp.zeros_like(field[:, :, :1])
    grad_c = jnp.concatenate([field[:, :, 1:] - field[:, :, :-1], zero_c], axis=2)
    return jnp.stack([grad_t, grad_r, grad_c], axis=0)

def divergence(dual):
    part_t = dual[0] - jnp.pad(dual[0], ((1, 0), (0, 0), (0, 0)))[:-1]
    part_r = dual[1] - jnp.pad(dual[1], ((0, 0), (1, 0), (0, 0)))[:, :-1]
    part_c = dual[2] - jnp.pad(dual[2], ((0, 0), (0, 0), (1, 0)))[:, :, :-1]
    return part_t + part_r + part_c

def reference(observed, kernel):
    kern = kernel / lax.optimization_barrier(jnp.sum(kernel, axis=0))
    theta = primal_step * tv_weight
    current = observed
    extrap = observed
    data_dual = jnp.zeros_like(observed)
    tv_dual = jnp.zeros((3,) + observed.shape, jnp.float32)
    for step in range(ITERS):
        data_dual = (data_dual + dual_step * (blur_forward(extrap, kern) - observed)) / (1.0 + dual_step)
        moved = current - primal_step * blur_adjoint(data_dual, kern)
        for inner in range(PASSES):
            target = divergence(tv_dual) - moved / theta
            trial = tv_dual + inner_step * gradient(target)
            length = jnp.sqrt(trial[0] * trial[0] + trial[1] * trial[1] + trial[2] * trial[2])
            tv_dual = trial / jnp.maximum(1.0, length)
        updated = moved - theta * divergence(tv_dual)
        extrap = 2.0 * updated - current
        current = updated
    return current
```

```python
import jax
import jax.numpy as jnp
from jax import lax
from jax.experimental import pallas as pl
from jax.experimental.pallas import tpu as pltpu
from jax.sharding import PartitionSpec as P

theta = 0.1
inner_step = 1.0 / 12.0
scale = -inner_step / theta

REACH = 2
BLOCK = 10
PAIR = ((0, 1), (1, 0))


def blur_kernel(u_ref, near_ref, far_ref, kernel_ref, v_ref, strip_ref, edge_ref, upad, fwd, adj, q, vflat):
    tm, row, col = lax.axis_index("tm"), lax.axis_index("row"), lax.axis_index("col")
    frames, rows, cols = u_ref.shape
    taps = kernel_ref.shape[0]
    half = taps // 2
    halo = 2 * half + REACH
    span = frames + 2 * REACH
    deep = v_ref.shape[1]

    odd = lax.rem(tm, 2)
    upad[halo : halo + frames] = u_ref[...]
    upad[pl.ds((1 - odd) * (halo + frames), halo)] = near_ref[...]
    upad[pl.ds(odd * (halo + frames), halo)] = far_ref[...]

    total = kernel_ref[0]
    for tap in range(1, taps):
        total = total + kernel_ref[tap]
    inverse = 1.0 / total
    for tap in range(taps):
        share = kernel_ref[tap] * inverse
        adj[tap] = share
        fwd[tap] = (share - 1.0 if tap == half else share) * (1.0 / 3.0)

    q_count = frames + 2 * (half + REACH)

    def forward(step, carry):
        base = step * BLOCK
        window = [upad[base + i] for i in range(BLOCK + taps - 1)]
        acc = [None] * BLOCK
        for tap in range(taps):
            weight = fwd[tap]
            for i in range(BLOCK):
                term = weight * window[i + tap]
                acc[i] = term if tap == 0 else acc[i] + term
        for i in range(BLOCK):
            q[base + i] = acc[i]
        return carry

    lax.fori_loop(0, q_count // BLOCK, forward, 0)
    nothing = jnp.zeros((half + REACH, rows, cols), jnp.float32)

    @pl.when(tm == 0)
    def _():
        q[: half + REACH] = nothing

    @pl.when(tm == lax.axis_size("tm") - 1)
    def _():
        q[q_count - half - REACH : q_count] = nothing

    q[q_count:] = jnp.zeros((q.shape[0] - q_count, rows, cols), jnp.float32)

    def adjoint(step, carry):
        base = step * BLOCK
        window = [q[base + i] for i in range(BLOCK + taps - 1)]
        acc = [None] * BLOCK
        for tap in range(taps):
            weight = adj[tap]
            for i in range(BLOCK):
                term = weight * window[i + taps - 1 - tap]
                acc[i] = term if tap == 0 else acc[i] + term
        for i in range(BLOCK):
            at = pl.multiple_of((base + i) * rows, rows)
            vflat[pl.ds(at, rows)] = upad[base + i + 2 * half] - acc[i]
        return carry

    steps = -(-span // BLOCK)
    lax.fori_loop(0, steps, adjoint, 0)
    vflat[steps * BLOCK * rows :] = jnp.zeros((vflat.shape[0] - steps * BLOCK * rows, cols), jnp.float32)

    lane = lax.broadcasted_iota(jnp.int32, (deep, cols), 1)
    edge = jnp.zeros((deep, cols), jnp.float32)
    for r in range(rows):
        plane = vflat[pl.ds(r, deep, stride=rows)]
        v_ref[r] = plane
        first = 4 * (r + 2 * row)
        moved = pltpu.roll(plane, first + 2, axis=1)
        low = first + 2 * col
        edge = jnp.where((lane >= low) & (lane < low + 2), moved, edge)
    edge_ref[...] = edge
    begin = (rows - 2) * (1 - row)
    strip_ref[0] = v_ref[begin]
    strip_ref[1] = v_ref[begin + 1]


def unit(z_t, z_r, z_c):
    factor = lax.rsqrt(jnp.maximum(1.0, z_t * z_t + z_r * z_r + z_c * z_c))
    return z_t * factor, z_r * factor, z_c * factor


def tv_kernel(v_ref, strip_ref, side_ref, corner_ref, out_ref, w, p_t, p_r, p_c, e_w, e_t, e_c):
    tm, row, col = lax.axis_index("tm"), lax.axis_index("row"), lax.axis_index("col")
    rows, deep, cols = v_ref.shape
    frames = out_ref.shape[0] // rows
    wide = rows + REACH

    lane = lax.broadcasted_iota(jnp.int32, (deep, cols), 1)
    time = lax.broadcasted_iota(jnp.int32, (deep, cols), 0)
    ends = ((tm == 0) & (time == REACH - 1)) | (
        (tm == lax.axis_size("tm") - 1) & (time == frames + REACH - 1)
    )
    keep_t = jnp.where(ends, 0.0, 1.0)
    keep_c = jnp.where((col == 1) & (lane == cols - 1), 0.0, 1.0)
    last, first = lane == cols - 1, lane == 0
    keep_r = jnp.where(lane < 4 * (wide - 1), 1.0, 0.0)
    is_right = jnp.where(col == 1, 1.0, 0.0)

    own = REACH * row
    foreign = rows * (1 - row)
    for r in range(rows):
        w[r + own, :deep] = v_ref[r] * scale
    for i in range(REACH):
        w[foreign + i, :deep] = strip_ref[i] * scale
    w[wide, :deep] = w[wide - 1, :deep]

    low = 4 * foreign
    corner = pltpu.roll(corner_ref[...], jnp.where(row == 0, 24, cols - 24), axis=1)
    edge = side_ref[...] + jnp.where((lane >= low) & (lane < low + 8), corner, 0.0)
    edge = edge * scale
    for r in range(wide):
        moved = pltpu.roll(w[r, :deep], 4 * r + 2, axis=1)
        begin = 4 * r + 2 * col
        edge = jnp.where((lane >= begin) & (lane < begin + 2), moved, edge)

    def edge_slopes(field):
        e_w[:deep] = field
        g_t = (e_w[1 : deep + 1] - field) * keep_t
        g_r = (pltpu.roll(field, cols - 4, axis=1) - field) * keep_r
        g_c = pltpu.roll(field, cols - 1, axis=1) - field
        return g_t, g_r, g_c

    e1 = unit(*edge_slopes(edge))
    e_t[8 : deep + 8] = e1[0]
    edge_div = e1[0] - e_t[7 : deep + 7] + e1[1] - pltpu.roll(e1[1], 4, axis=1) + e1[2] - pltpu.roll(e1[2], 1, axis=1)
    edge2 = edge_div * inner_step + edge
    slopes2 = edge_slopes(edge2)
    e2 = unit(e1[0] + slopes2[0], e1[1] + slopes2[1], e1[2] + slopes2[2])
    e_c[0] = edge
    e_c[1] = e1[2] * is_right
    e_c[2] = edge2
    e_c[3] = e2[2] * is_right

    def slopes(r, which):
        here = w[r, :deep]
        g_t = (w[r, 1 : deep + 1] - here) * keep_t
        g_r = w[r + 1, :deep] - here
        right = jnp.where(last, pltpu.roll(e_c[which], cols - 3 - 4 * r, axis=1), pltpu.roll(here, cols - 1, axis=1))
        return g_t, g_r, (right - here) * keep_c

    def store(r, p):
        p_t[r, 8 : deep + 8] = p[0]
        p_r[r + 1] = p[1]
        p_c[r] = p[2]

    def divergence(r, which):
        here = p_c[r]
        left = jnp.where(first, pltpu.roll(e_c[which], cols - 1 - 4 * r, axis=1), pltpu.roll(here, 1, axis=1))
        return p_t[r, 8 : deep + 8] - p_t[r, 7 : deep + 7] + p_r[r + 1] - p_r[r] + here - left

    p_r[0] = jnp.zeros((deep, cols), jnp.float32)

    def first_pass(r, carry):
        store(r, unit(*slopes(r, 0)))
        return carry

    def second_w(r, carry):
        w[r, :deep] = divergence(r, 1) * inner_step + w[r, :deep]
        return carry

    def second_pass(r, carry):
        g_t, g_r, g_c = slopes(r, 2)
        store(r, unit(p_t[r, 8 : deep + 8] + g_t, p_r[r + 1] + g_r, p_c[r] + g_c))
        return carry

    lax.fori_loop(0, wide, first_pass, 0)
    lax.fori_loop(0, wide, second_w, 0)
    w[wide, :deep] = w[wide - 1, :deep]
    lax.fori_loop(0, wide, second_pass, 0)
    for r in range(rows):
        updated = v_ref[r] - theta * divergence(r + own, 3)
        p_c[r + own] = updated
        out_ref[pl.ds(r, frames, stride=rows)] = p_c[r + own, REACH : REACH + frames]


def body(observed, kernel):
    frames, rows, cols = observed.shape
    taps = kernel.shape[0]
    half = taps // 2
    halo = 2 * half + REACH
    deep = -(-(frames + 2 * REACH) // 8) * 8
    count = lax.axis_size("tm")
    odd = lax.axis_index("tm") % 2
    vmem = pl.BlockSpec(memory_space=pltpu.VMEM)
    f32 = jnp.float32

    near = lax.dynamic_slice_in_dim(observed, (1 - odd) * (frames - halo), halo, axis=0)
    far = lax.dynamic_slice_in_dim(observed, odd * (frames - halo), halo, axis=0)
    far = lax.ppermute(far, "tm", [(i, i + 1 if i % 2 else i - 1) for i in range(1, count - 1)])
    near = lax.ppermute(near, "tm", [(i, i ^ 1) for i in range(count)])

    v, strip, edge = pl.pallas_call(
        blur_kernel,
        out_shape=(
            jax.ShapeDtypeStruct((rows, deep, cols), f32),
            jax.ShapeDtypeStruct((REACH, deep, cols), f32),
            jax.ShapeDtypeStruct((deep, cols), f32),
        ),
        in_specs=[vmem] * 4,
        out_specs=(vmem,) * 3,
        scratch_shapes=[
            pltpu.VMEM((frames + 2 * halo, rows, cols), f32),
            pltpu.VMEM((taps, rows, cols), f32),
            pltpu.VMEM((taps, rows, cols), f32),
            pltpu.VMEM((deep + 2 * half, rows, cols), f32),
            pltpu.VMEM((deep * rows, cols), f32),
        ],
        name="blur",
    )(observed, near, far, kernel)

    strip = lax.ppermute(strip, "row", PAIR)
    side = lax.ppermute(edge, "col", PAIR)
    corner = lax.ppermute(edge, ("row", "col"), [(0, 3), (3, 0), (1, 2), (2, 1)])

    wide = rows + REACH
    out = pl.pallas_call(
        tv_kernel,
        out_shape=jax.ShapeDtypeStruct((frames * rows, cols), f32),
        in_specs=[vmem] * 4,
        out_specs=vmem,
        scratch_shapes=[
            pltpu.VMEM((wide + 1, deep + 8, cols), f32),
            pltpu.VMEM((wide, deep + 8, cols), f32),
            pltpu.VMEM((wide + 1, deep, cols), f32),
            pltpu.VMEM((wide, deep, cols), f32),
            pltpu.VMEM((deep + 8, cols), f32),
            pltpu.VMEM((deep + 8, cols), f32),
            pltpu.VMEM((4, deep, cols), f32),
        ],
        name="tv",
    )(v, strip, side, corner)
    return out.reshape(frames, rows, cols)


def solution(mesh):
    in_specs = (P("tm", "row", "col"), P(None, "row", "col"))
    out_specs = P("tm", "row", "col")
    return jax.shard_map(body, mesh=mesh, in_specs=in_specs, out_specs=out_specs, check_vma=False)
```

```python
import jax
import jax.numpy as jnp
from jax import lax
from jax.experimental import pallas as pl
from jax.experimental.pallas import tpu as pltpu
from jax.sharding import PartitionSpec as P

theta = 0.1
inner_step = 1.0 / 12.0
scale = -inner_step / theta

REACH = 2
BLOCK = 10
PAIR = ((0, 1), (1, 0))


def blur_kernel(u_ref, near_ref, far_ref, kernel_ref, v_ref, strip_ref, edge_ref, upad, fwd, adj, q, vflat):
    tm, row, col = lax.axis_index("tm"), lax.axis_index("row"), lax.axis_index("col")
    frames, rows, cols = u_ref.shape
    taps = kernel_ref.shape[0]
    half = taps // 2
    halo = 2 * half + REACH
    span = frames + 2 * REACH
    deep = v_ref.shape[1]

    odd = lax.rem(tm, 2)
    upad[halo : halo + frames] = u_ref[...]
    upad[pl.ds((1 - odd) * (halo + frames), halo)] = near_ref[...]
    upad[pl.ds(odd * (halo + frames), halo)] = far_ref[...]

    total = kernel_ref[0]
    for tap in range(1, taps):
        total = total + kernel_ref[tap]
    inverse = 1.0 / total
    for tap in range(taps):
        share = kernel_ref[tap] * inverse
        adj[tap] = share
        fwd[tap] = (share - 1.0 if tap == half else share) * (1.0 / 3.0)

    q_count = frames + 2 * (half + REACH)

    def forward(step, carry):
        base = step * BLOCK
        window = [upad[base + i] for i in range(BLOCK + taps - 1)]
        acc = [None] * BLOCK
        for tap in range(taps):
            weight = fwd[tap]
            for i in range(BLOCK):
                term = weight * window[i + tap]
                acc[i] = term if tap == 0 else acc[i] + term
        for i in range(BLOCK):
            q[base + i] = acc[i]
        return carry

    lax.fori_loop(0, q_count // BLOCK, forward, 0)
    nothing = jnp.zeros((half + REACH, rows, cols), jnp.float32)

    @pl.when(tm == 0)
    def _():
        q[: half + REACH] = nothing

    @pl.when(tm == lax.axis_size("tm") - 1)
    def _():
        q[q_count - half - REACH : q_count] = nothing

    q[q_count:] = jnp.zeros((q.shape[0] - q_count, rows, cols), jnp.float32)

    def adjoint(step, carry):
        base = step * BLOCK
        window = [q[base + i] for i in range(BLOCK + taps - 1)]
        acc = [None] * BLOCK
        for tap in range(taps):
            weight = adj[tap]
            for i in range(BLOCK):
                term = weight * window[i + taps - 1 - tap]
                acc[i] = term if tap == 0 else acc[i] + term
        for i in range(BLOCK):
            at = pl.multiple_of((base + i) * rows, rows)
            vflat[pl.ds(at, rows)] = upad[base + i + 2 * half] - acc[i]
        return carry

    steps = -(-span // BLOCK)
    lax.fori_loop(0, steps, adjoint, 0)
    vflat[steps * BLOCK * rows :] = jnp.zeros((vflat.shape[0] - steps * BLOCK * rows, cols), jnp.float32)

    lane = lax.broadcasted_iota(jnp.int32, (deep, cols), 1)
    edge = jnp.zeros((deep, cols), jnp.float32)
    for r in range(rows):
        plane = vflat[pl.ds(r, deep, stride=rows)]
        v_ref[r] = plane
        first = 4 * (r + 2 * row)
        moved = pltpu.roll(plane, first + 2, axis=1)
        low = first + 2 * col
        edge = jnp.where((lane >= low) & (lane < low + 2), moved, edge)
    edge_ref[...] = edge
    begin = (rows - 2) * (1 - row)
    strip_ref[0] = v_ref[begin]
    strip_ref[1] = v_ref[begin + 1]


def unit(z_t, z_r, z_c):
    factor = lax.rsqrt(jnp.maximum(1.0, z_t * z_t + z_r * z_r + z_c * z_c))
    return z_t * factor, z_r * factor, z_c * factor


def tv_kernel(v_ref, strip_ref, side_ref, corner_ref, out_ref, w, p_t, p_r, p_c, e_w, e_t, e_c):
    tm, row, col = lax.axis_index("tm"), lax.axis_index("row"), lax.axis_index("col")
    rows, deep, cols = v_ref.shape
    frames = out_ref.shape[0] // rows
    wide = rows + REACH

    lane = lax.broadcasted_iota(jnp.int32, (deep, cols), 1)
    time = lax.broadcasted_iota(jnp.int32, (deep, cols), 0)
    ends = ((tm == 0) & (time == REACH - 1)) | (
        (tm == lax.axis_size("tm") - 1) & (time == frames + REACH - 1)
    )
    keep_t = jnp.where(ends, 0.0, 1.0)
    keep_c = jnp.where((col == 1) & (lane == cols - 1), 0.0, 1.0)
    last, first = lane == cols - 1, lane == 0
    keep_r = jnp.where(lane < 4 * (wide - 1), 1.0, 0.0)
    is_right = jnp.where(col == 1, 1.0, 0.0)

    own = REACH * row
    foreign = rows * (1 - row)
    for r in range(rows):
        w[r + own, :deep] = v_ref[r] * scale
    for i in range(REACH):
        w[foreign + i, :deep] = strip_ref[i] * scale
    w[wide, :deep] = w[wide - 1, :deep]

    low = 4 * foreign
    corner = pltpu.roll(corner_ref[...], jnp.where(row == 0, 24, cols - 24), axis=1)
    edge = side_ref[...] + jnp.where((lane >= low) & (lane < low + 8), corner, 0.0)
    edge = edge * scale
    for r in range(wide):
        moved = pltpu.roll(w[r, :deep], 4 * r + 2, axis=1)
        begin = 4 * r + 2 * col
        edge = jnp.where((lane >= begin) & (lane < begin + 2), moved, edge)

    def edge_slopes(field):
        e_w[:deep] = field
        g_t = (e_w[1 : deep + 1] - field) * keep_t
        g_r = (pltpu.roll(field, cols - 4, axis=1) - field) * keep_r
        g_c = pltpu.roll(field, cols - 1, axis=1) - field
        return g_t, g_r, g_c

    e1 = unit(*edge_slopes(edge))
    e_t[8 : deep + 8] = e1[0]
    edge_div = e1[0] - e_t[7 : deep + 7] + e1[1] - pltpu.roll(e1[1], 4, axis=1) + e1[2] - pltpu.roll(e1[2], 1, axis=1)
    edge2 = edge_div * inner_step + edge
    slopes2 = edge_slopes(edge2)
    e2 = unit(e1[0] + slopes2[0], e1[1] + slopes2[1], e1[2] + slopes2[2])
    e_c[0] = edge
    e_c[1] = e1[2] * is_right
    e_c[2] = edge2
    e_c[3] = e2[2] * is_right

    def slopes(r, which):
        here = w[r, :deep]
        g_t = (w[r, 1 : deep + 1] - here) * keep_t
        g_r = w[r + 1, :deep] - here
        right = jnp.where(last, pltpu.roll(e_c[which], cols - 3 - 4 * r, axis=1), pltpu.roll(here, cols - 1, axis=1))
        return g_t, g_r, (right - here) * keep_c

    def store(r, p):
        p_t[r, 8 : deep + 8] = p[0]
        p_r[r + 1] = p[1]
        p_c[r] = p[2]

    def divergence(r, which):
        here = p_c[r]
        left = jnp.where(first, pltpu.roll(e_c[which], cols - 1 - 4 * r, axis=1), pltpu.roll(here, 1, axis=1))
        return p_t[r, 8 : deep + 8] - p_t[r, 7 : deep + 7] + p_r[r + 1] - p_r[r] + here - left

    p_r[0] = jnp.zeros((deep, cols), jnp.float32)

    def first_pass(r, carry):
        store(r, unit(*slopes(r, 0)))
        return carry

    def second_w(r, carry):
        w[r, :deep] = divergence(r, 1) * inner_step + w[r, :deep]
        return carry

    def second_pass(r, carry):
        g_t, g_r, g_c = slopes(r, 2)
        store(r, unit(p_t[r, 8 : deep + 8] + g_t, p_r[r + 1] + g_r, p_c[r] + g_c))
        return carry

    lax.fori_loop(0, wide, first_pass, 0)
    lax.fori_loop(0, wide, second_w, 0)
    w[wide, :deep] = w[wide - 1, :deep]
    lax.fori_loop(0, wide, second_pass, 0)
    for r in range(rows):
        updated = v_ref[r] - theta * divergence(r + own, 3)
        p_c[r + own] = updated
        out_ref[pl.ds(r, frames, stride=rows)] = p_c[r + own, REACH : REACH + frames]


def on_chip(x):
    return pltpu.with_memory_space_constraint(x, pltpu.VMEM)


def body(observed, kernel):
    frames, rows, cols = observed.shape
    taps = kernel.shape[0]
    half = taps // 2
    halo = 2 * half + REACH
    deep = -(-(frames + 2 * REACH) // 8) * 8
    count = lax.axis_size("tm")
    odd = lax.axis_index("tm") % 2
    vmem = pl.BlockSpec(memory_space=pltpu.VMEM)
    f32 = jnp.float32

    near = lax.dynamic_slice_in_dim(observed, (1 - odd) * (frames - halo), halo, axis=0)
    far = lax.dynamic_slice_in_dim(observed, odd * (frames - halo), halo, axis=0)
    far = lax.ppermute(far, "tm", [(i, i + 1 if i % 2 else i - 1) for i in range(1, count - 1)])
    near = lax.ppermute(near, "tm", [(i, i ^ 1) for i in range(count)])

    v, strip, edge = pl.pallas_call(
        blur_kernel,
        out_shape=(
            pltpu.VMEM((rows, deep, cols), f32),
            pltpu.VMEM((REACH, deep, cols), f32),
            pltpu.VMEM((deep, cols), f32),
        ),
        in_specs=[vmem] * 4,
        out_specs=(vmem,) * 3,
        scratch_shapes=[
            pltpu.VMEM((frames + 2 * halo, rows, cols), f32),
            pltpu.VMEM((taps, rows, cols), f32),
            pltpu.VMEM((taps, rows, cols), f32),
            pltpu.VMEM((deep + 2 * half, rows, cols), f32),
            pltpu.VMEM((deep * rows, cols), f32),
        ],
        name="blur",
    )(*map(on_chip, (observed, near, far, kernel)))

    strip = lax.ppermute(strip, "row", PAIR)
    side = lax.ppermute(edge, "col", PAIR)
    corner = lax.ppermute(edge, ("row", "col"), [(0, 3), (3, 0), (1, 2), (2, 1)])

    wide = rows + REACH
    out = pl.pallas_call(
        tv_kernel,
        out_shape=jax.ShapeDtypeStruct((frames * rows, cols), f32),
        in_specs=[vmem] * 4,
        out_specs=vmem,
        scratch_shapes=[
            pltpu.VMEM((wide + 1, deep + 8, cols), f32),
            pltpu.VMEM((wide, deep + 8, cols), f32),
            pltpu.VMEM((wide + 1, deep, cols), f32),
            pltpu.VMEM((wide, deep, cols), f32),
            pltpu.VMEM((deep + 8, cols), f32),
            pltpu.VMEM((deep + 8, cols), f32),
            pltpu.VMEM((4, deep, cols), f32),
        ],
        name="tv",
    )(*map(on_chip, (v, strip, side, corner)))
    return out.reshape(frames, rows, cols)


def solution(mesh):
    in_specs = (P("tm", "row", "col"), P(None, "row", "col"))
    out_specs = P("tm", "row", "col")
    return jax.shard_map(body, mesh=mesh, in_specs=in_specs, out_specs=out_specs, check_vma=False)
```

```python
import jax
import jax.numpy as jnp
from jax import lax
from jax.experimental import pallas as pl
from jax.experimental.pallas import tpu as pltpu
from jax.sharding import PartitionSpec as P

theta = 0.1
inner_step = 1.0 / 12.0
scale = -inner_step / theta

REACH = 2
BLOCK = 10


def blur_kernel(u_ref, near_ref, far_ref, kernel_ref, v_ref, message_ref, upad, fwd, adj, q, vflat):
    tm, row, col = lax.axis_index("tm"), lax.axis_index("row"), lax.axis_index("col")
    frames, rows, cols = u_ref.shape
    taps = kernel_ref.shape[0]
    half = taps // 2
    halo = 2 * half + REACH
    span = frames + 2 * REACH
    deep = v_ref.shape[1]

    odd = lax.rem(tm, 2)
    upad[halo : halo + frames] = u_ref[...]
    upad[pl.ds((1 - odd) * (halo + frames), halo)] = near_ref[...]
    upad[pl.ds(odd * (halo + frames), halo)] = far_ref[...]

    total = kernel_ref[0]
    for tap in range(1, taps):
        total = total + kernel_ref[tap]
    inverse = 1.0 / total
    for tap in range(taps):
        share = kernel_ref[tap] * inverse
        adj[tap] = share
        fwd[tap] = (share - 1.0 if tap == half else share) * (1.0 / 3.0)

    q_count = frames + 2 * (half + REACH)

    def forward(step, carry):
        base = step * BLOCK
        window = [upad[base + i] for i in range(BLOCK + taps - 1)]
        acc = [None] * BLOCK
        for tap in range(taps):
            weight = fwd[tap]
            for i in range(BLOCK):
                term = weight * window[i + tap]
                acc[i] = term if tap == 0 else acc[i] + term
        for i in range(BLOCK):
            q[base + i] = acc[i]
        return carry

    lax.fori_loop(0, q_count // BLOCK, forward, 0)
    nothing = jnp.zeros((half + REACH, rows, cols), jnp.float32)

    @pl.when(tm == 0)
    def _():
        q[: half + REACH] = nothing

    @pl.when(tm == lax.axis_size("tm") - 1)
    def _():
        q[q_count - half - REACH : q_count] = nothing

    q[q_count:] = jnp.zeros((q.shape[0] - q_count, rows, cols), jnp.float32)

    def adjoint(step, carry):
        base = step * BLOCK
        window = [q[base + i] for i in range(BLOCK + taps - 1)]
        acc = [None] * BLOCK
        for tap in range(taps):
            weight = adj[tap]
            for i in range(BLOCK):
                term = weight * window[i + taps - 1 - tap]
                acc[i] = term if tap == 0 else acc[i] + term
        for i in range(BLOCK):
            at = pl.multiple_of((base + i) * rows, rows)
            vflat[pl.ds(at, rows)] = upad[base + i + 2 * half] - acc[i]
        return carry

    steps = -(-span // BLOCK)
    lax.fori_loop(0, steps, adjoint, 0)
    vflat[steps * BLOCK * rows :] = jnp.zeros((vflat.shape[0] - steps * BLOCK * rows, cols), jnp.float32)

    lane = lax.broadcasted_iota(jnp.int32, (deep, cols), 1)
    edge = jnp.zeros((deep, cols), jnp.float32)
    for r in range(rows):
        plane = vflat[pl.ds(r, deep, stride=rows)]
        v_ref[r] = plane
        first = 4 * (r + 2 * row)
        moved = pltpu.roll(plane, first + 2, axis=1)
        low = first + 2 * col
        edge = jnp.where((lane >= low) & (lane < low + 2), moved, edge)
    third = deep // 3
    packed = edge[:third] + pltpu.roll(edge[third : 2 * third], 40, axis=1) + pltpu.roll(edge[2 * third :], 80, axis=1)
    message_ref[2 * row + (1 - col), :third] = packed
    message_ref[2 * (1 - row) + (1 - col), :third] = packed
    begin = (rows - REACH) * (1 - row)
    for i in range(REACH):
        message_ref[2 * (1 - row) + col, i * deep : (i + 1) * deep] = v_ref[begin + i]


def unit(z_t, z_r, z_c):
    factor = lax.rsqrt(jnp.maximum(1.0, z_t * z_t + z_r * z_r + z_c * z_c))
    return z_t * factor, z_r * factor, z_c * factor


def unpacked(packed):
    lane = lax.broadcasted_iota(jnp.int32, packed.shape, 1)
    parts = [packed, pltpu.roll(packed, 88, axis=1), pltpu.roll(packed, 48, axis=1)]
    return jnp.concatenate([jnp.where(lane < 40, part, 0.0) for part in parts], axis=0)


def tv_kernel(v_ref, got_ref, out_ref, w, p_t, p_r, p_c, e_w, e_t, e_c):
    tm, row, col = lax.axis_index("tm"), lax.axis_index("row"), lax.axis_index("col")
    rows, deep, cols = v_ref.shape
    frames = out_ref.shape[0] // rows
    wide = rows + REACH

    lane = lax.broadcasted_iota(jnp.int32, (deep, cols), 1)
    time = lax.broadcasted_iota(jnp.int32, (deep, cols), 0)
    ends = ((tm == 0) & (time == REACH - 1)) | (
        (tm == lax.axis_size("tm") - 1) & (time == frames + REACH - 1)
    )
    keep_t = jnp.where(ends, 0.0, 1.0)
    keep_c = jnp.where((col == 1) & (lane == cols - 1), 0.0, 1.0)
    last, first = lane == cols - 1, lane == 0
    keep_r = jnp.where(lane < 4 * (wide - 1), 1.0, 0.0)
    is_right = jnp.where(col == 1, 1.0, 0.0)

    own = REACH * row
    foreign = rows * (1 - row)
    for r in range(rows):
        w[r + own, :deep] = v_ref[r] * scale
    for i in range(REACH):
        w[foreign + i, :deep] = got_ref[2 * (1 - row) + col, i * deep : (i + 1) * deep] * scale
    w[wide, :deep] = w[wide - 1, :deep]

    low = 4 * foreign
    corner = pltpu.roll(unpacked(got_ref[2 * (1 - row) + (1 - col), : deep // 3]), jnp.where(row == 0, 24, cols - 24), axis=1)
    edge = unpacked(got_ref[2 * row + (1 - col), : deep // 3]) + jnp.where((lane >= low) & (lane < low + 8), corner, 0.0)
    edge = edge * scale
    for r in range(wide):
        moved = pltpu.roll(w[r, :deep], 4 * r + 2, axis=1)
        begin = 4 * r + 2 * col
        edge = jnp.where((lane >= begin) & (lane < begin + 2), moved, edge)

    def edge_slopes(field):
        e_w[:deep] = field
        g_t = (e_w[1 : deep + 1] - field) * keep_t
        g_r = (pltpu.roll(field, cols - 4, axis=1) - field) * keep_r
        g_c = pltpu.roll(field, cols - 1, axis=1) - field
        return g_t, g_r, g_c

    e1 = unit(*edge_slopes(edge))
    e_t[8 : deep + 8] = e1[0]
    edge_div = e1[0] - e_t[7 : deep + 7] + e1[1] - pltpu.roll(e1[1], 4, axis=1) + e1[2] - pltpu.roll(e1[2], 1, axis=1)
    edge2 = edge_div * inner_step + edge
    slopes2 = edge_slopes(edge2)
    e2 = unit(e1[0] + slopes2[0], e1[1] + slopes2[1], e1[2] + slopes2[2])
    e_c[0] = edge
    e_c[1] = e1[2] * is_right
    e_c[2] = edge2
    e_c[3] = e2[2] * is_right

    def slopes(r, which):
        here = w[r, :deep]
        g_t = (w[r, 1 : deep + 1] - here) * keep_t
        g_r = w[r + 1, :deep] - here
        right = jnp.where(last, pltpu.roll(e_c[which], cols - 3 - 4 * r, axis=1), pltpu.roll(here, cols - 1, axis=1))
        return g_t, g_r, (right - here) * keep_c

    def store(r, p):
        p_t[r, 8 : deep + 8] = p[0]
        p_r[r + 1] = p[1]
        p_c[r] = p[2]

    def divergence(r, which):
        here = p_c[r]
        left = jnp.where(first, pltpu.roll(e_c[which], cols - 1 - 4 * r, axis=1), pltpu.roll(here, 1, axis=1))
        return p_t[r, 8 : deep + 8] - p_t[r, 7 : deep + 7] + p_r[r + 1] - p_r[r] + here - left

    p_r[0] = jnp.zeros((deep, cols), jnp.float32)

    def first_pass(r):
        store(r, unit(*slopes(r, 0)))

    def second_w(r):
        w[r, :deep] = divergence(r, 1) * inner_step + w[r, :deep]

    def second_pass(r):
        g_t, g_r, g_c = slopes(r, 2)
        store(r, unit(p_t[r, 8 : deep + 8] + g_t, p_r[r + 1] + g_r, p_c[r] + g_c))

    for r in range(wide):
        first_pass(r)
    for r in range(wide):
        second_w(r)
    w[wide, :deep] = w[wide - 1, :deep]
    for r in range(wide):
        second_pass(r)
    for r in range(rows):
        updated = v_ref[r] - theta * divergence(r + own, 3)
        p_c[r + own] = updated
        out_ref[pl.ds(r, frames, stride=rows)] = p_c[r + own, REACH : REACH + frames]


def on_chip(x):
    return pltpu.with_memory_space_constraint(x, pltpu.VMEM)


def on_chip_result(shape):
    return pltpu.VMEM(shape, jnp.float32)


def body(observed, kernel):
    frames, rows, cols = observed.shape
    taps = kernel.shape[0]
    half = taps // 2
    halo = 2 * half + REACH
    deep = -(-(frames + 2 * REACH) // 8) * 8
    count = lax.axis_size("tm")
    odd = lax.axis_index("tm") % 2
    vmem = pl.BlockSpec(memory_space=pltpu.VMEM)
    f32 = jnp.float32

    near = lax.dynamic_slice_in_dim(observed, (1 - odd) * (frames - halo), halo, axis=0)
    far = lax.dynamic_slice_in_dim(observed, odd * (frames - halo), halo, axis=0)
    far = lax.ppermute(far, "tm", [(i, i + 1 if i % 2 else i - 1) for i in range(1, count - 1)])
    near = lax.ppermute(near, "tm", [(i, i ^ 1) for i in range(count)])

    v, message = pl.pallas_call(
        blur_kernel,
        out_shape=(
            on_chip_result((rows, deep, cols)),
            on_chip_result((4, REACH * deep, cols)),
        ),
        in_specs=[vmem] * 4,
        out_specs=(vmem,) * 2,
        scratch_shapes=[
            pltpu.VMEM((frames + 2 * halo, rows, cols), f32),
            pltpu.VMEM((taps, rows, cols), f32),
            pltpu.VMEM((taps, rows, cols), f32),
            pltpu.VMEM((deep + 2 * half, rows, cols), f32),
            pltpu.VMEM((deep * rows, cols), f32),
        ],
        name="blur",
    )(*map(on_chip, (observed, near, far, kernel)))

    got = lax.all_to_all(message, ("row", "col"), 0, 0, tiled=True)

    wide = rows + REACH
    out = pl.pallas_call(
        tv_kernel,
        out_shape=jax.ShapeDtypeStruct((frames * rows, cols), f32),
        in_specs=[vmem] * 2,
        out_specs=vmem,
        scratch_shapes=[
            pltpu.VMEM((wide + 1, deep + 8, cols), f32),
            pltpu.VMEM((wide, deep + 8, cols), f32),
            pltpu.VMEM((wide + 1, deep, cols), f32),
            pltpu.VMEM((wide, deep, cols), f32),
            pltpu.VMEM((deep + 8, cols), f32),
            pltpu.VMEM((deep + 8, cols), f32),
            pltpu.VMEM((4, deep, cols), f32),
        ],
        name="tv",
    )(*map(on_chip, (v, got)))
    return out.reshape(frames, rows, cols)


def solution(mesh):
    in_specs = (P("tm", "row", "col"), P(None, "row", "col"))
    out_specs = P("tm", "row", "col")
    return jax.shard_map(body, mesh=mesh, in_specs=in_specs, out_specs=out_specs, check_vma=False)
```

```python
import jax
import jax.numpy as jnp
from jax import lax
from jax.experimental import pallas as pl
from jax.experimental.pallas import tpu as pltpu
from jax.sharding import PartitionSpec as P

theta = 0.1
inner_step = 1.0 / 12.0
scale = -inner_step / theta

REACH = 2
BLOCK = 10


def edge_lanes(planes, row, col):
    edge = jnp.zeros_like(planes[0])
    lane = lax.broadcasted_iota(jnp.int32, edge.shape, 1)
    for r, plane in enumerate(planes):
        first = 4 * (r + REACH * row)
        low = first + 2 * col
        edge = jnp.where((lane >= low) & (lane < low + 2), pltpu.roll(plane, first + 2, axis=1), edge)
    return edge


def border(ref, count, rows, row, col):
    begin = (rows - REACH) * (1 - row)
    planes = [ref[pl.ds(r, count, stride=rows)] for r in range(rows)]
    strips = [ref[pl.ds(begin + i, count, stride=rows)] for i in range(REACH)]
    return strips + [edge_lanes(planes, row, col)]


def weights_kernel(u_ref, kernel_ref, fwd_ref, adj_ref, border_u, border_fwd, border_adj):
    row, col = lax.axis_index("row"), lax.axis_index("col")
    frames, cols = border_u.shape[1:]
    rows = u_ref.shape[0] // frames
    taps = kernel_ref.shape[0] // rows
    half = taps // 2
    third = 1.0 / 3.0
    total = kernel_ref[pl.ds(0, rows)]
    for tap in range(1, taps):
        total = total + kernel_ref[pl.ds(tap * rows, rows)]
    inverse = 1.0 / total
    for tap in range(taps):
        share = kernel_ref[pl.ds(tap * rows, rows)] * inverse
        adj_ref[pl.ds(tap * rows, rows)] = share
        fwd_ref[pl.ds(tap * rows, rows)] = (share - 1.0 if tap == half else share) * third
    center = jnp.where(lax.broadcasted_iota(jnp.int32, (taps, cols), 0) == half, third, 0.0)
    for i, plane in enumerate(border(adj_ref, taps, rows, row, col)):
        border_adj[i, :taps] = plane
        border_fwd[i, :taps] = plane * third - center
    for i, plane in enumerate(border(u_ref, frames, rows, row, col)):
        border_u[i] = plane


def border_kernel(near_ref, far_ref, border_u, border_fwd, border_adj, message_ref, u, q, v, packed, sems):
    tm, row, col = lax.axis_index("tm"), lax.axis_index("row"), lax.axis_index("col")
    planes, frames, cols = border_u.shape
    taps = 2 * (q.shape[1] - v.shape[1]) // 2 + 1
    half = taps // 2
    halo = 2 * half + REACH
    rows = near_ref.shape[0] // halo
    deep = v.shape[1]
    length = q.shape[1]

    odd = lax.rem(tm, 2) == 1
    near = border(near_ref, halo, rows, row, col)
    far = border(far_ref, halo, rows, row, col)
    for i in range(planes):
        u[i, :halo] = jnp.where(odd, near[i], far[i])
        u[i, halo : halo + frames] = border_u[i]
        u[i, halo + frames : frames + 2 * halo] = jnp.where(odd, far[i], near[i])
        u[i, frames + 2 * halo :] = jnp.zeros((u.shape[1] - frames - 2 * halo, cols), jnp.float32)

    def forward(i):
        acc = [None] * (length // 8)
        for tap in range(taps):
            weight = jnp.broadcast_to(border_fwd[i, tap : tap + 1], (8, cols))
            for c in range(length // 8):
                term = weight * u[i, 8 * c + tap : 8 * c + tap + 8]
                acc[c] = term if tap == 0 else acc[c] + term
        for c in range(length // 8):
            q[i, 8 * c : 8 * c + 8] = acc[c]

    def close(begin, end):
        nothing = jnp.zeros((end - begin, half + REACH, cols), jnp.float32)

        @pl.when(tm == 0)
        def _():
            q[begin:end, : half + REACH] = nothing

        @pl.when(tm == lax.axis_size("tm") - 1)
        def _():
            q[begin:end, q_count - half - REACH : q_count] = nothing

    def adjoint(i):
        acc = [None] * (deep // 8)
        for tap in range(taps):
            weight = jnp.broadcast_to(border_adj[i, tap : tap + 1], (8, cols))
            for c in range(deep // 8):
                at = 8 * c + 2 * half - tap
                term = weight * q[i, at : at + 8]
                acc[c] = term if tap == 0 else acc[c] + term
        for c in range(deep // 8):
            v[i, 8 * c : 8 * c + 8] = u[i, 8 * c + 2 * half : 8 * c + 2 * half + 8] - acc[c]

    q_count = frames + 2 * (half + REACH)
    across, beside, corner = 2 * (1 - row) + col, 2 * row + (1 - col), 2 * (1 - row) + (1 - col)
    third = deep // 3
    copies = [
        pltpu.make_async_copy(v.at[0], message_ref.at[across, pl.ds(0, deep)], sems.at[0]),
        pltpu.make_async_copy(v.at[1], message_ref.at[across, pl.ds(deep, deep)], sems.at[1]),
        pltpu.make_async_copy(packed, message_ref.at[beside, pl.ds(0, third)], sems.at[2]),
        pltpu.make_async_copy(packed, message_ref.at[corner, pl.ds(0, third)], sems.at[3]),
    ]
    for i in range(REACH):
        forward(i)
    close(0, REACH)
    for i in range(REACH):
        adjoint(i)
        copies[i].start()
    forward(REACH)
    close(REACH, planes)
    adjoint(REACH)
    edge = v[REACH]
    packed[...] = edge[:third] + pltpu.roll(edge[third : 2 * third], 40, axis=1) + pltpu.roll(edge[2 * third :], 80, axis=1)
    copies[2].start()
    copies[3].start()
    for copy in copies:
        copy.wait()


def blur_kernel(u_ref, near_ref, far_ref, fwd, adj, v_ref, upad, q, vflat):
    tm = lax.axis_index("tm")
    rows, deep, cols = v_ref.shape
    taps = fwd.shape[0] // rows
    frames = u_ref.shape[0] // rows
    half = taps // 2
    halo = 2 * half + REACH
    span = frames + 2 * REACH

    def at(frame, count=1):
        return pl.ds(pl.multiple_of(frame * rows, rows), count * rows)

    odd = lax.rem(tm, 2)
    upad[at(halo, frames)] = u_ref[...]
    upad[at((1 - odd) * (halo + frames), halo)] = near_ref[...]
    upad[at(odd * (halo + frames), halo)] = far_ref[...]

    q_count = frames + 2 * (half + REACH)

    def forward(step, carry):
        base = step * BLOCK
        window = [upad[at(base + i)] for i in range(BLOCK + taps - 1)]
        acc = [None] * BLOCK
        for tap in range(taps):
            weight = fwd[at(tap)]
            for i in range(BLOCK):
                term = weight * window[i + tap]
                acc[i] = term if tap == 0 else acc[i] + term
        for i in range(BLOCK):
            q[at(base + i)] = acc[i]
        return carry

    lax.fori_loop(0, q_count // BLOCK, forward, 0)
    nothing = jnp.zeros(((half + REACH) * rows, cols), jnp.float32)

    @pl.when(tm == 0)
    def _():
        q[at(0, half + REACH)] = nothing

    @pl.when(tm == lax.axis_size("tm") - 1)
    def _():
        q[at(q_count - half - REACH, half + REACH)] = nothing

    q[q_count * rows :] = jnp.zeros((q.shape[0] - q_count * rows, cols), jnp.float32)

    def adjoint(step, carry):
        base = step * BLOCK
        window = [q[at(base + i)] for i in range(BLOCK + taps - 1)]
        acc = [None] * BLOCK
        for tap in range(taps):
            weight = adj[at(tap)]
            for i in range(BLOCK):
                term = weight * window[i + taps - 1 - tap]
                acc[i] = term if tap == 0 else acc[i] + term
        for i in range(BLOCK):
            vflat[at(base + i)] = upad[at(base + i + 2 * half)] - acc[i]
        return carry

    steps = -(-span // BLOCK)
    lax.fori_loop(0, steps, adjoint, 0)
    vflat[steps * BLOCK * rows :] = jnp.zeros((vflat.shape[0] - steps * BLOCK * rows, cols), jnp.float32)

    for r in range(rows):
        v_ref[r] = vflat[pl.ds(r, deep, stride=rows)]


def unit(z_t, z_r, z_c):
    factor = lax.rsqrt(jnp.maximum(1.0, z_t * z_t + z_r * z_r + z_c * z_c))
    return z_t * factor, z_r * factor, z_c * factor


def unpacked(packed):
    lane = lax.broadcasted_iota(jnp.int32, packed.shape, 1)
    parts = [packed, pltpu.roll(packed, 88, axis=1), pltpu.roll(packed, 48, axis=1)]
    return jnp.concatenate([jnp.where(lane < 40, part, 0.0) for part in parts], axis=0)


def tv_kernel(v_ref, got_ref, out_ref, w, p_t, p_r, p_c, e_w, e_t, e_c):
    tm, row, col = lax.axis_index("tm"), lax.axis_index("row"), lax.axis_index("col")
    rows, deep, cols = v_ref.shape
    frames = out_ref.shape[0] // rows
    wide = rows + REACH

    lane = lax.broadcasted_iota(jnp.int32, (deep, cols), 1)
    time = lax.broadcasted_iota(jnp.int32, (deep, cols), 0)
    ends = ((tm == 0) & (time == REACH - 1)) | (
        (tm == lax.axis_size("tm") - 1) & (time == frames + REACH - 1)
    )
    keep_t = jnp.where(ends, 0.0, 1.0)
    keep_c = jnp.where((col == 1) & (lane == cols - 1), 0.0, 1.0)
    last, first = lane == cols - 1, lane == 0
    keep_r = jnp.where(lane < 4 * (wide - 1), 1.0, 0.0)
    is_right = jnp.where(col == 1, 1.0, 0.0)

    own = REACH * row
    foreign = rows * (1 - row)
    for r in range(rows):
        w[r + own, :deep] = v_ref[r] * scale
    for i in range(REACH):
        w[foreign + i, :deep] = got_ref[2 * (1 - row) + col, i * deep : (i + 1) * deep] * scale
    w[wide, :deep] = w[wide - 1, :deep]

    low = 4 * foreign
    corner = pltpu.roll(unpacked(got_ref[2 * (1 - row) + (1 - col), : deep // 3]), jnp.where(row == 0, 24, cols - 24), axis=1)
    edge = unpacked(got_ref[2 * row + (1 - col), : deep // 3]) + jnp.where((lane >= low) & (lane < low + 8), corner, 0.0)
    edge = edge * scale
    for r in range(wide):
        moved = pltpu.roll(w[r, :deep], 4 * r + 2, axis=1)
        begin = 4 * r + 2 * col
        edge = jnp.where((lane >= begin) & (lane < begin + 2), moved, edge)

    def edge_slopes(field):
        e_w[:deep] = field
        g_t = (e_w[1 : deep + 1] - field) * keep_t
        g_r = (pltpu.roll(field, cols - 4, axis=1) - field) * keep_r
        g_c = pltpu.roll(field, cols - 1, axis=1) - field
        return g_t, g_r, g_c

    e1 = unit(*edge_slopes(edge))
    e_t[8 : deep + 8] = e1[0]
    edge_div = e1[0] - e_t[7 : deep + 7] + e1[1] - pltpu.roll(e1[1], 4, axis=1) + e1[2] - pltpu.roll(e1[2], 1, axis=1)
    edge2 = edge_div * inner_step + edge
    slopes2 = edge_slopes(edge2)
    e2 = unit(e1[0] + slopes2[0], e1[1] + slopes2[1], e1[2] + slopes2[2])
    e_c[0] = edge
    e_c[1] = e1[2] * is_right
    e_c[2] = edge2
    e_c[3] = e2[2] * is_right

    def slopes(r, which):
        here = w[r, :deep]
        g_t = (w[r, 1 : deep + 1] - here) * keep_t
        g_r = w[r + 1, :deep] - here
        right = jnp.where(last, pltpu.roll(e_c[which], cols - 3 - 4 * r, axis=1), pltpu.roll(here, cols - 1, axis=1))
        return g_t, g_r, (right - here) * keep_c

    def store(r, p):
        p_t[r, 8 : deep + 8] = p[0]
        p_r[r + 1] = p[1]
        p_c[r] = p[2]

    def divergence(r, which):
        here = p_c[r]
        left = jnp.where(first, pltpu.roll(e_c[which], cols - 1 - 4 * r, axis=1), pltpu.roll(here, 1, axis=1))
        return p_t[r, 8 : deep + 8] - p_t[r, 7 : deep + 7] + p_r[r + 1] - p_r[r] + here - left

    p_r[0] = jnp.zeros((deep, cols), jnp.float32)

    def first_pass(r):
        store(r, unit(*slopes(r, 0)))

    def second_w(r):
        w[r, :deep] = divergence(r, 1) * inner_step + w[r, :deep]

    def second_pass(r):
        g_t, g_r, g_c = slopes(r, 2)
        store(r, unit(p_t[r, 8 : deep + 8] + g_t, p_r[r + 1] + g_r, p_c[r] + g_c))

    for r in range(wide):
        first_pass(r)
    for r in range(wide):
        second_w(r)
    w[wide, :deep] = w[wide - 1, :deep]
    for r in range(wide):
        second_pass(r)
    for r in range(rows):
        updated = v_ref[r] - theta * divergence(r + own, 3)
        p_c[r + own] = updated
        out_ref[pl.ds(r, frames, stride=rows)] = p_c[r + own, REACH : REACH + frames]


def on_chip(x):
    return pltpu.with_memory_space_constraint(x, pltpu.VMEM)


def on_chip_result(shape):
    return pltpu.VMEM(shape, jnp.float32)


def body(observed, kernel):
    frames, rows, cols = observed.shape
    taps = kernel.shape[0]
    half = taps // 2
    halo = 2 * half + REACH
    deep = -(-(frames + 2 * REACH) // 8) * 8
    count = lax.axis_size("tm")
    odd = lax.axis_index("tm") % 2
    vmem = pl.BlockSpec(memory_space=pltpu.VMEM)
    f32 = jnp.float32

    near = lax.dynamic_slice_in_dim(observed, (1 - odd) * (frames - halo), halo, axis=0).reshape(halo * rows, cols)
    far = lax.dynamic_slice_in_dim(observed, odd * (frames - halo), halo, axis=0).reshape(halo * rows, cols)
    far = lax.ppermute(far, "tm", [(i, i + 1 if i % 2 else i - 1) for i in range(1, count - 1)])
    near = lax.ppermute(near, "tm", [(i, i ^ 1) for i in range(count)])
    near, far = on_chip(near), on_chip(far)
    mine = on_chip(observed.reshape(frames * rows, cols))

    planes = REACH + 1
    padded_taps = -(-taps // 8) * 8
    fwd, adj, border_u, border_fwd, border_adj = pl.pallas_call(
        weights_kernel,
        out_shape=(
            on_chip_result((taps * rows, cols)),
            on_chip_result((taps * rows, cols)),
            on_chip_result((planes, frames, cols)),
            on_chip_result((planes, padded_taps, cols)),
            on_chip_result((planes, padded_taps, cols)),
        ),
        in_specs=[vmem] * 2,
        out_specs=(vmem,) * 5,
        name="weights",
    )(mine, on_chip(kernel.reshape(taps * rows, cols)))
    fwd, adj, border_u, border_fwd, border_adj = map(on_chip, (fwd, adj, border_u, border_fwd, border_adj))

    length = deep + 2 * half
    message = pl.pallas_call(
        border_kernel,
        out_shape=jax.ShapeDtypeStruct((4, REACH * deep, cols), f32),
        in_specs=[vmem] * 5,
        out_specs=pl.BlockSpec(memory_space=pl.ANY),
        scratch_shapes=[
            pltpu.VMEM((planes, length + 2 * half, cols), f32),
            pltpu.VMEM((planes, length, cols), f32),
            pltpu.VMEM((planes, deep, cols), f32),
            pltpu.VMEM((deep // 3, cols), f32),
            pltpu.SemaphoreType.DMA((4,)),
        ],
        name="border",
    )(near, far, border_u, border_fwd, border_adj)
    v = pl.pallas_call(
        blur_kernel,
        out_shape=on_chip_result((rows, deep, cols)),
        in_specs=[vmem] * 5,
        out_specs=vmem,
        scratch_shapes=[
            pltpu.VMEM(((frames + 2 * halo) * rows, cols), f32),
            pltpu.VMEM(((deep + 2 * half) * rows, cols), f32),
            pltpu.VMEM((deep * rows, cols), f32),
        ],
        cost_estimate=pl.CostEstimate(flops=2 * taps * (2 * deep + 2 * half) * rows * cols, bytes_accessed=0, transcendentals=0),
        name="blur",
    )(mine, near, far, fwd, adj)
    got = lax.all_to_all(message, ("row", "col"), 0, 0, tiled=True)

    wide = rows + REACH
    out = pl.pallas_call(
        tv_kernel,
        out_shape=jax.ShapeDtypeStruct((frames * rows, cols), f32),
        in_specs=[vmem] * 2,
        out_specs=vmem,
        scratch_shapes=[
            pltpu.VMEM((wide + 1, deep + 8, cols), f32),
            pltpu.VMEM((wide, deep + 8, cols), f32),
            pltpu.VMEM((wide + 1, deep, cols), f32),
            pltpu.VMEM((wide, deep, cols), f32),
            pltpu.VMEM((deep + 8, cols), f32),
            pltpu.VMEM((deep + 8, cols), f32),
            pltpu.VMEM((4, deep, cols), f32),
        ],
        name="tv",
    )(*map(on_chip, (v, got)))
    return out.reshape(frames, rows, cols)


def solution(mesh):
    in_specs = (P("tm", "row", "col"), P(None, "row", "col"))
    out_specs = P("tm", "row", "col")
    return jax.shard_map(body, mesh=mesh, in_specs=in_specs, out_specs=out_specs, check_vma=False)
```

```python
import jax
import jax.numpy as jnp
from jax import lax
from jax.experimental import pallas as pl
from jax.experimental.pallas import tpu as pltpu
from jax.sharding import PartitionSpec as P

theta = 0.1
inner_step = 1.0 / 12.0
scale = -inner_step / theta

REACH = 2
ROWS = 8
HALF = 36
BLOCK, WIDE_BLOCK = 10, 12


def at(frame, count=1):
    return pl.ds(pl.multiple_of(frame * ROWS, ROWS), count * ROWS)


def blur(weights, field, begin, block, flip=False):
    taps = weights.shape[0] // ROWS
    window = [field[at(begin + i)] for i in range(block + taps - 1)]
    acc = [None] * block
    for tap in range(taps):
        weight = weights[at(tap)]
        for i in range(block):
            term = weight * window[i + (taps - 1 - tap if flip else tap)]
            acc[i] = term if tap == 0 else acc[i] + term
    return acc


def own_kernel(u_ref, kernel_ref, fwd, adj, q_ref):
    taps = kernel_ref.shape[0] // ROWS
    half = taps // 2
    total = kernel_ref[at(0)]
    for tap in range(1, taps):
        total = total + kernel_ref[at(tap)]
    inverse = 1.0 / total
    for tap in range(taps):
        share = kernel_ref[at(tap)] * inverse
        adj[at(tap)] = share
        fwd[at(tap)] = (share - 1.0 if tap == half else share) * (1.0 / 3.0)

    def forward(step, carry):
        for i, value in enumerate(blur(fwd, u_ref, 1 + step * BLOCK, BLOCK)):
            q_ref[at(step * BLOCK + i)] = value
        return carry

    lax.fori_loop(0, q_ref.shape[0] // ROWS // BLOCK, forward, 0)


def half_blur(side, part_ref, u_ref, q_own, fwd, adj, u, q, v, v_begin):
    frames = u_ref.shape[0] // ROWS
    halo = part_ref.shape[0] // ROWS
    half = (halo - REACH) // 2
    u[at(side * halo, halo)] = part_ref[...]
    u[at((1 - side) * halo, halo)] = u_ref[at(side * (frames - halo), halo)]
    q[at(halo + 1, q_own.shape[0] // ROWS)] = q_own[...]

    def forward(step, carry):
        for i, value in enumerate(blur(fwd, u, step * WIDE_BLOCK, WIDE_BLOCK)):
            q[at(side * frames + step * WIDE_BLOCK + i)] = value
        return carry

    lax.fori_loop(0, HALF // WIDE_BLOCK, forward, 0)
    tm = lax.axis_index("tm")
    nothing = jnp.zeros(((half + REACH) * ROWS, q.shape[1]), jnp.float32)

    @pl.when((tm == 0) & (side == 0))
    def _():
        q[at(0, half + REACH)] = nothing

    @pl.when((tm == lax.axis_size("tm") - 1) & (side == 1))
    def _():
        q[at(frames + half + REACH, half + REACH)] = nothing

    def adjoint(step, carry):
        base = step * WIDE_BLOCK
        for i, value in enumerate(blur(adj, q, side * 2 * half + base, WIDE_BLOCK, True)):
            v[at(v_begin + base + i)] = u[at((1 - side) * 2 * half + base + i)] - value
        return carry

    lax.fori_loop(0, HALF // WIDE_BLOCK, adjoint, 0)


def far_kernel(part_ref, u_ref, q_own, fwd, adj, q_ref, v_ref, u, q):
    side = lax.rem(lax.axis_index("tm"), 2)
    frames = u_ref.shape[0] // ROWS
    half_blur(side, part_ref, u_ref, q_own, fwd, adj, u, q, v_ref, 0)
    q_ref[...] = q[at(side * frames, HALF)]


def near_kernel(part_ref, u_ref, q_own, fwd, adj, q_far, v_far, v_ref, message_ref, u, q, vflat):
    row, col = lax.axis_index("row"), lax.axis_index("col")
    side = 1 - lax.rem(lax.axis_index("tm"), 2)
    frames = u_ref.shape[0] // ROWS
    halo = part_ref.shape[0] // ROWS
    rows, deep, cols = v_ref.shape
    span = frames + 2 * REACH
    q[at((1 - side) * frames, HALF)] = q_far[...]
    vflat[at((1 - side) * (span - HALF), HALF)] = v_far[...]
    half_blur(side, part_ref, u_ref, q_own, fwd, adj, u, q, vflat, side * (span - HALF))
    vflat[at(span, deep - span)] = jnp.zeros(((deep - span) * rows, cols), jnp.float32)

    lane = lax.broadcasted_iota(jnp.int32, (deep, cols), 1)
    edge = jnp.zeros((deep, cols), jnp.float32)
    for r in range(rows):
        plane = vflat[pl.ds(r, deep, stride=rows)]
        v_ref[r] = plane
        first = 4 * (r + 2 * row)
        moved = pltpu.roll(plane, first + 2, axis=1)
        low = first + 2 * col
        edge = jnp.where((lane >= low) & (lane < low + 2), moved, edge)
    third = deep // 3
    packed = edge[:third] + pltpu.roll(edge[third : 2 * third], 40, axis=1) + pltpu.roll(edge[2 * third :], 80, axis=1)
    message_ref[2 * row + (1 - col), :third] = packed
    message_ref[2 * (1 - row) + (1 - col), :third] = packed
    begin = (rows - REACH) * (1 - row)
    for i in range(REACH):
        message_ref[2 * (1 - row) + col, i * deep : (i + 1) * deep] = v_ref[begin + i]


def unit(z_t, z_r, z_c):
    factor = lax.rsqrt(jnp.maximum(1.0, z_t * z_t + z_r * z_r + z_c * z_c))
    return z_t * factor, z_r * factor, z_c * factor


def unpacked(packed):
    lane = lax.broadcasted_iota(jnp.int32, packed.shape, 1)
    parts = [packed, pltpu.roll(packed, 88, axis=1), pltpu.roll(packed, 48, axis=1)]
    return jnp.concatenate([jnp.where(lane < 40, part, 0.0) for part in parts], axis=0)


def tv_kernel(v_ref, got_ref, out_ref, w, p_t, p_r, p_c, e_w, e_t, e_c):
    tm, row, col = lax.axis_index("tm"), lax.axis_index("row"), lax.axis_index("col")
    rows, deep, cols = v_ref.shape
    frames = out_ref.shape[0] // rows
    wide = rows + REACH

    lane = lax.broadcasted_iota(jnp.int32, (deep, cols), 1)
    time = lax.broadcasted_iota(jnp.int32, (deep, cols), 0)
    ends = ((tm == 0) & (time == REACH - 1)) | (
        (tm == lax.axis_size("tm") - 1) & (time == frames + REACH - 1)
    )
    keep_t = jnp.where(ends, 0.0, 1.0)
    keep_c = jnp.where((col == 1) & (lane == cols - 1), 0.0, 1.0)
    last, first = lane == cols - 1, lane == 0
    keep_r = jnp.where(lane < 4 * (wide - 1), 1.0, 0.0)
    is_right = jnp.where(col == 1, 1.0, 0.0)

    own = REACH * row
    foreign = rows * (1 - row)
    for r in range(rows):
        w[r + own, :deep] = v_ref[r] * scale
    for i in range(REACH):
        w[foreign + i, :deep] = got_ref[2 * (1 - row) + col, i * deep : (i + 1) * deep] * scale
    w[wide, :deep] = w[wide - 1, :deep]

    low = 4 * foreign
    corner = pltpu.roll(unpacked(got_ref[2 * (1 - row) + (1 - col), : deep // 3]), jnp.where(row == 0, 24, cols - 24), axis=1)
    edge = unpacked(got_ref[2 * row + (1 - col), : deep // 3]) + jnp.where((lane >= low) & (lane < low + 8), corner, 0.0)
    edge = edge * scale
    for r in range(wide):
        moved = pltpu.roll(w[r, :deep], 4 * r + 2, axis=1)
        begin = 4 * r + 2 * col
        edge = jnp.where((lane >= begin) & (lane < begin + 2), moved, edge)

    def edge_slopes(field):
        e_w[:deep] = field
        g_t = (e_w[1 : deep + 1] - field) * keep_t
        g_r = (pltpu.roll(field, cols - 4, axis=1) - field) * keep_r
        g_c = pltpu.roll(field, cols - 1, axis=1) - field
        return g_t, g_r, g_c

    e1 = unit(*edge_slopes(edge))
    e_t[8 : deep + 8] = e1[0]
    edge_div = e1[0] - e_t[7 : deep + 7] + e1[1] - pltpu.roll(e1[1], 4, axis=1) + e1[2] - pltpu.roll(e1[2], 1, axis=1)
    edge2 = edge_div * inner_step + edge
    slopes2 = edge_slopes(edge2)
    e2 = unit(e1[0] + slopes2[0], e1[1] + slopes2[1], e1[2] + slopes2[2])
    e_c[0] = edge
    e_c[1] = e1[2] * is_right
    e_c[2] = edge2
    e_c[3] = e2[2] * is_right

    def slopes(r, which):
        here = w[r, :deep]
        g_t = (w[r, 1 : deep + 1] - here) * keep_t
        g_r = w[r + 1, :deep] - here
        right = jnp.where(last, pltpu.roll(e_c[which], cols - 3 - 4 * r, axis=1), pltpu.roll(here, cols - 1, axis=1))
        return g_t, g_r, (right - here) * keep_c

    def store(r, p):
        p_t[r, 8 : deep + 8] = p[0]
        p_r[r + 1] = p[1]
        p_c[r] = p[2]

    def divergence(r, which):
        here = p_c[r]
        left = jnp.where(first, pltpu.roll(e_c[which], cols - 1 - 4 * r, axis=1), pltpu.roll(here, 1, axis=1))
        return p_t[r, 8 : deep + 8] - p_t[r, 7 : deep + 7] + p_r[r + 1] - p_r[r] + here - left

    p_r[0] = jnp.zeros((deep, cols), jnp.float32)

    def first_pass(r):
        store(r, unit(*slopes(r, 0)))

    def second_w(r):
        w[r, :deep] = divergence(r, 1) * inner_step + w[r, :deep]

    def second_pass(r):
        g_t, g_r, g_c = slopes(r, 2)
        store(r, unit(p_t[r, 8 : deep + 8] + g_t, p_r[r + 1] + g_r, p_c[r] + g_c))

    for r in range(wide):
        first_pass(r)
    for r in range(wide):
        second_w(r)
    w[wide, :deep] = w[wide - 1, :deep]
    for r in range(wide):
        second_pass(r)
    for r in range(rows):
        updated = v_ref[r] - theta * divergence(r + own, 3)
        p_c[r + own] = updated
        out_ref[pl.ds(r, frames, stride=rows)] = p_c[r + own, REACH : REACH + frames]


def on_chip(x):
    return pltpu.with_memory_space_constraint(x, pltpu.VMEM)


def on_chip_result(shape):
    return pltpu.VMEM(shape, jnp.float32)


def body(observed, kernel):
    frames, rows, cols = observed.shape
    taps = kernel.shape[0]
    half = taps // 2
    halo = 2 * half + REACH
    deep = -(-(frames + 2 * REACH) // 8) * 8
    count = lax.axis_size("tm")
    odd = lax.axis_index("tm") % 2
    vmem = pl.BlockSpec(memory_space=pltpu.VMEM)
    f32 = jnp.float32

    near = lax.dynamic_slice_in_dim(observed, (1 - odd) * (frames - halo), halo, axis=0).reshape(halo * rows, cols)
    far = lax.dynamic_slice_in_dim(observed, odd * (frames - halo), halo, axis=0).reshape(halo * rows, cols)
    far = lax.ppermute(far, "tm", [(i, i + 1 if i % 2 else i - 1) for i in range(1, count - 1)])
    near = lax.ppermute(near, "tm", [(i, i ^ 1) for i in range(count)])
    near, far = on_chip(near), on_chip(far)
    mine = on_chip(observed.reshape(frames * rows, cols))

    def flat(count):
        return (count * rows, cols)

    fwd, adj, q_own = pl.pallas_call(
        own_kernel,
        out_shape=(on_chip_result(flat(taps)), on_chip_result(flat(taps)), on_chip_result(flat(frames - 2 * half - 2))),
        in_specs=[vmem] * 2,
        out_specs=(vmem,) * 3,
        name="own",
    )(mine, on_chip(kernel.reshape(taps * rows, cols)))
    fwd, adj, q_own = map(on_chip, (fwd, adj, q_own))
    q_far, v_far = pl.pallas_call(
        far_kernel,
        out_shape=(on_chip_result(flat(HALF)),) * 2,
        in_specs=[vmem] * 5,
        out_specs=(vmem,) * 2,
        scratch_shapes=[pltpu.VMEM(flat(2 * halo), f32), pltpu.VMEM(flat(deep + 2 * half), f32)],
        name="far",
    )(far, mine, q_own, fwd, adj)
    v, message = pl.pallas_call(
        near_kernel,
        out_shape=(on_chip_result((rows, deep, cols)), on_chip_result((4, REACH * deep, cols))),
        in_specs=[vmem] * 7,
        out_specs=(vmem,) * 2,
        scratch_shapes=[
            pltpu.VMEM(flat(2 * halo), f32),
            pltpu.VMEM(flat(deep + 2 * half), f32),
            pltpu.VMEM(flat(deep), f32),
        ],
        name="near",
    )(near, mine, q_own, fwd, adj, on_chip(q_far), on_chip(v_far))
    got = lax.all_to_all(message, ("row", "col"), 0, 0, tiled=True)

    wide = rows + REACH
    out = pl.pallas_call(
        tv_kernel,
        out_shape=jax.ShapeDtypeStruct((frames * rows, cols), f32),
        in_specs=[vmem] * 2,
        out_specs=vmem,
        scratch_shapes=[
            pltpu.VMEM((wide + 1, deep + 8, cols), f32),
            pltpu.VMEM((wide, deep + 8, cols), f32),
            pltpu.VMEM((wide + 1, deep, cols), f32),
            pltpu.VMEM((wide, deep, cols), f32),
            pltpu.VMEM((deep + 8, cols), f32),
            pltpu.VMEM((deep + 8, cols), f32),
            pltpu.VMEM((4, deep, cols), f32),
        ],
        name="tv",
    )(*map(on_chip, (v, got)))
    return out.reshape(frames, rows, cols)


def solution(mesh):
    in_specs = (P("tm", "row", "col"), P(None, "row", "col"))
    out_specs = P("tm", "row", "col")
    return jax.shard_map(body, mesh=mesh, in_specs=in_specs, out_specs=out_specs, check_vma=False)
```

```python
import jax
import jax.numpy as jnp
from jax import lax
from jax.experimental import pallas as pl
from jax.experimental.pallas import tpu as pltpu
from jax.sharding import PartitionSpec as P

theta = 0.1
inner_step = 1.0 / 12.0
scale = -inner_step / theta

REACH = 2
ROWS = 8
HALF = 36
BLOCK, PAIRS = 10, 6


def at(frame, count=1):
    return pl.ds(pl.multiple_of(frame * ROWS, ROWS), count * ROWS)


def blur(weights, field, begin, block):
    taps = weights.shape[0] // ROWS
    window = [field[at(begin + i)] for i in range(block + taps - 1)]
    acc = [None] * block
    for tap in range(taps):
        weight = weights[at(tap)]
        for i in range(block):
            term = weight * window[i + tap]
            acc[i] = term if tap == 0 else acc[i] + term
    return acc


def blur_pairs(weights, sums, field, begin, shape, pairs, finish):
    less, more = shape
    taps = weights.shape[0] // ROWS
    half = taps // 2
    count = pairs + half
    for t in range(count):
        low, high = field[at(begin + 2 * t)], field[at(begin + 2 * t + 1)]
        less[at(t)] = low - high
        if t + 1 < count:
            more[at(t)] = field[at(begin + 2 * t + 2)] - high

    def step(number, carry):
        base = number * PAIRS
        first, shared, last = [None] * PAIRS, [None] * PAIRS, [None] * PAIRS
        for k in range(half + 1):
            even, both = weights[at(2 * k)], sums[at(k)]
            odd = weights[at(2 * k + 1)] if k < half else None
            for i in range(PAIRS):
                term = even * less[at(base + i + k)]
                first[i] = first[i] + term if k else term
                term = both * field[at(begin + 2 * (base + i + k) + 1)]
                shared[i] = shared[i] + term if k else term
                if k < half:
                    term = odd * more[at(base + i + k)]
                    last[i] = last[i] + term if k else term
        for i in range(PAIRS):
            finish(2 * (base + i), first[i] + shared[i])
            finish(2 * (base + i) + 1, last[i] + shared[i])
        return carry

    lax.fori_loop(0, pairs // PAIRS, step, 0)


def own_kernel(u_ref, kernel_ref, fwd, adj, fwd_sums, adj_sums, q_ref):
    taps = kernel_ref.shape[0] // ROWS
    half = taps // 2
    total = kernel_ref[at(0)]
    for tap in range(1, taps):
        total = total + kernel_ref[at(tap)]
    inverse = 1.0 / total
    for tap in range(taps):
        share = kernel_ref[at(tap)] * inverse
        adj[at(taps - 1 - tap)] = share
        fwd[at(tap)] = (share - 1.0 if tap == half else share) * (1.0 / 3.0)
    for weights, sums in ((fwd, fwd_sums), (adj, adj_sums)):
        for k in range(half):
            sums[at(k)] = weights[at(2 * k)] + weights[at(2 * k + 1)]
        sums[at(half)] = weights[at(taps - 1)]

    def forward(step, carry):
        for i, value in enumerate(blur(fwd, u_ref, 1 + step * BLOCK, BLOCK)):
            q_ref[at(step * BLOCK + i)] = value
        return carry

    lax.fori_loop(0, q_ref.shape[0] // ROWS // BLOCK, forward, 0)


def half_blur(side, part_ref, u_ref, q_own, taps_of, u, q, less, more, v, v_begin):
    fwd, adj, fwd_sums, adj_sums = taps_of
    frames = u_ref.shape[0] // ROWS
    halo = part_ref.shape[0] // ROWS
    half = (halo - REACH) // 2
    u[at(side * halo, halo)] = part_ref[...]
    u[at((1 - side) * halo, halo)] = u_ref[at(side * (frames - halo), halo)]
    q[at(halo + 1, q_own.shape[0] // ROWS)] = q_own[...]

    def keep_q(i, value):
        q[at(side * frames + i)] = value

    blur_pairs(fwd, fwd_sums, u, 0, (less, more), HALF // 2, keep_q)
    tm = lax.axis_index("tm")
    nothing = jnp.zeros(((half + REACH) * ROWS, q.shape[1]), jnp.float32)

    @pl.when((tm == 0) & (side == 0))
    def _():
        q[at(0, half + REACH)] = nothing

    @pl.when((tm == lax.axis_size("tm") - 1) & (side == 1))
    def _():
        q[at(frames + half + REACH, half + REACH)] = nothing

    def keep_v(i, value):
        v[at(v_begin + i)] = u[at((1 - side) * 2 * half + i)] - value

    blur_pairs(adj, adj_sums, q, side * 2 * half, (less, more), HALF // 2, keep_v)


def far_kernel(part_ref, u_ref, q_own, fwd, adj, fwd_sums, adj_sums, q_ref, v_ref, u, q, less, more):
    side = lax.rem(lax.axis_index("tm"), 2)
    frames = u_ref.shape[0] // ROWS
    half_blur(side, part_ref, u_ref, q_own, (fwd, adj, fwd_sums, adj_sums), u, q, less, more, v_ref, 0)
    q_ref[...] = q[at(side * frames, HALF)]


def near_kernel(
    part_ref, u_ref, q_own, fwd, adj, fwd_sums, adj_sums, q_far, v_far, vflat, edge_ref, message_ref, u, q, less, more
):
    row, col = lax.axis_index("row"), lax.axis_index("col")
    side = 1 - lax.rem(lax.axis_index("tm"), 2)
    frames = u_ref.shape[0] // ROWS
    halo = part_ref.shape[0] // ROWS
    deep, cols = edge_ref.shape
    rows = vflat.shape[0] // deep
    span = frames + 2 * REACH
    q[at((1 - side) * frames, HALF)] = q_far[...]
    vflat[at((1 - side) * (span - HALF), HALF)] = v_far[...]
    taps_of = (fwd, adj, fwd_sums, adj_sums)
    half_blur(side, part_ref, u_ref, q_own, taps_of, u, q, less, more, vflat, side * (span - HALF))
    vflat[at(span, deep - span)] = jnp.zeros(((deep - span) * rows, cols), jnp.float32)

    lane = lax.broadcasted_iota(jnp.int32, (deep, cols), 1)
    edge = jnp.zeros((deep, cols), jnp.float32)
    for r in range(rows):
        plane = vflat[pl.ds(r, deep, stride=rows)]
        first = 4 * (r + 2 * row)
        moved = pltpu.roll(plane, first + 2, axis=1)
        low = first + 2 * col
        edge = jnp.where((lane >= low) & (lane < low + 2), moved, edge)
    edge_ref[...] = edge
    third = deep // 3
    packed = edge[:third] + pltpu.roll(edge[third : 2 * third], 40, axis=1) + pltpu.roll(edge[2 * third :], 80, axis=1)
    message_ref[2 * row + (1 - col), :third] = packed
    message_ref[2 * (1 - row) + (1 - col), :third] = packed
    begin = (rows - REACH) * (1 - row)
    for i in range(REACH):
        message_ref[2 * (1 - row) + col, i * span : (i + 1) * span] = vflat[pl.ds(begin + i, span, stride=rows)]


def unit(z_t, z_r, z_c):
    factor = lax.rsqrt(jnp.maximum(1.0, z_t * z_t + z_r * z_r + z_c * z_c))
    return z_t * factor, z_r * factor, z_c * factor


def unpacked(packed):
    lane = lax.broadcasted_iota(jnp.int32, packed.shape, 1)
    parts = [packed, pltpu.roll(packed, 88, axis=1), pltpu.roll(packed, 48, axis=1)]
    return jnp.concatenate([jnp.where(lane < 40, part, 0.0) for part in parts], axis=0)


def tv_kernel(v_ref, edge_ref, got_ref, out_ref, w, p_t, p_r, p_c, e_w, e_t, e_c):
    tm, row, col = lax.axis_index("tm"), lax.axis_index("row"), lax.axis_index("col")
    deep, cols = edge_ref.shape
    rows = v_ref.shape[0] // deep
    frames = out_ref.shape[0] // rows
    wide = rows + REACH
    span = frames + 2 * REACH

    lane = lax.broadcasted_iota(jnp.int32, (deep, cols), 1)
    time = lax.broadcasted_iota(jnp.int32, (deep, cols), 0)
    ends = ((tm == 0) & (time == REACH - 1)) | (
        (tm == lax.axis_size("tm") - 1) & (time == frames + REACH - 1)
    )
    keep_t = jnp.where(ends, 0.0, 1.0)
    keep_c = jnp.where((col == 1) & (lane == cols - 1), 0.0, 1.0)
    last, first = lane == cols - 1, lane == 0
    keep_r = jnp.where(lane < 4 * (wide - 1), 1.0, 0.0)
    is_right = jnp.where(col == 1, 1.0, 0.0)

    own = REACH * row
    foreign = rows * (1 - row)
    for r in range(rows):
        w[r + own, :deep] = v_ref[pl.ds(r, deep, stride=rows)] * scale
    for i in range(REACH):
        w[foreign + i, span:deep] = jnp.zeros((deep - span, cols), jnp.float32)
        w[foreign + i, :span] = got_ref[2 * (1 - row) + col, i * span : (i + 1) * span] * scale
    w[wide, :deep] = w[wide - 1, :deep]

    low = 4 * foreign
    corner = pltpu.roll(unpacked(got_ref[2 * (1 - row) + (1 - col), : deep // 3]), jnp.where(row == 0, 24, cols - 24), axis=1)
    edge = edge_ref[...] + unpacked(got_ref[2 * row + (1 - col), : deep // 3]) + jnp.where((lane >= low) & (lane < low + 8), corner, 0.0)
    edge = edge * scale
    for i in range(REACH):
        moved = pltpu.roll(w[foreign + i, :deep], 4 * (foreign + i) + 2, axis=1)
        begin = 4 * (foreign + i) + 2 * col
        edge = jnp.where((lane >= begin) & (lane < begin + 2), moved, edge)

    def edge_slopes(field):
        e_w[:deep] = field
        g_t = (e_w[1 : deep + 1] - field) * keep_t
        g_r = (pltpu.roll(field, cols - 4, axis=1) - field) * keep_r
        g_c = pltpu.roll(field, cols - 1, axis=1) - field
        return g_t, g_r, g_c

    e1 = unit(*edge_slopes(edge))
    e_t[8 : deep + 8] = e1[0]
    edge_div = e1[0] - e_t[7 : deep + 7] + e1[1] - pltpu.roll(e1[1], 4, axis=1) + e1[2] - pltpu.roll(e1[2], 1, axis=1)
    edge2 = edge_div * inner_step + edge
    slopes2 = edge_slopes(edge2)
    e2 = unit(e1[0] + slopes2[0], e1[1] + slopes2[1], e1[2] + slopes2[2])
    e_c[0] = edge
    e_c[1] = e1[2] * is_right
    e_c[2] = edge2
    e_c[3] = e2[2] * is_right

    def slopes(r, which):
        here = w[r, :deep]
        g_t = (w[r, 1 : deep + 1] - here) * keep_t
        g_r = w[r + 1, :deep] - here
        right = jnp.where(last, pltpu.roll(e_c[which], cols - 3 - 4 * r, axis=1), pltpu.roll(here, cols - 1, axis=1))
        return g_t, g_r, (right - here) * keep_c

    def store(r, p):
        p_t[r, 8 : deep + 8] = p[0]
        p_r[r + 1] = p[1]
        p_c[r] = p[2]

    def divergence(r, which):
        here = p_c[r]
        left = jnp.where(first, pltpu.roll(e_c[which], cols - 1 - 4 * r, axis=1), pltpu.roll(here, 1, axis=1))
        return p_t[r, 8 : deep + 8] - p_t[r, 7 : deep + 7] + p_r[r + 1] - p_r[r] + here - left

    p_r[0] = jnp.zeros((deep, cols), jnp.float32)

    def first_pass(r):
        store(r, unit(*slopes(r, 0)))

    def second_w(r):
        w[r, :deep] = divergence(r, 1) * inner_step + w[r, :deep]

    def second_pass(r):
        g_t, g_r, g_c = slopes(r, 2)
        store(r, unit(p_t[r, 8 : deep + 8] + g_t, p_r[r + 1] + g_r, p_c[r] + g_c))

    for r in range(wide):
        first_pass(r)
    for r in range(wide):
        second_w(r)
    w[wide, :deep] = w[wide - 1, :deep]
    for r in range(wide):
        second_pass(r)
    for r in range(rows):
        updated = v_ref[pl.ds(r, deep, stride=rows)] - theta * divergence(r + own, 3)
        p_c[r + own] = updated
        out_ref[pl.ds(r, frames, stride=rows)] = p_c[r + own, REACH : REACH + frames]


def on_chip(x):
    return pltpu.with_memory_space_constraint(x, pltpu.VMEM)


def on_chip_result(shape):
    return pltpu.VMEM(shape, jnp.float32)


def body(observed, kernel):
    frames, rows, cols = observed.shape
    taps = kernel.shape[0]
    half = taps // 2
    halo = 2 * half + REACH
    deep = -(-(frames + 2 * REACH) // 8) * 8
    count = lax.axis_size("tm")
    odd = lax.axis_index("tm") % 2
    vmem = pl.BlockSpec(memory_space=pltpu.VMEM)
    f32 = jnp.float32

    near = lax.dynamic_slice_in_dim(observed, (1 - odd) * (frames - halo), halo, axis=0).reshape(halo * rows, cols)
    far = lax.dynamic_slice_in_dim(observed, odd * (frames - halo), halo, axis=0).reshape(halo * rows, cols)
    far = lax.ppermute(far, "tm", [(i, i + 1 if i % 2 else i - 1) for i in range(1, count - 1)])
    near = lax.ppermute(near, "tm", [(i, i ^ 1) for i in range(count)])
    near, far = on_chip(near), on_chip(far)
    mine = on_chip(observed.reshape(frames * rows, cols))

    def flat(count):
        return (count * rows, cols)

    shapes = [flat(n) for n in (taps, taps, half + 1, half + 1, frames - 2 * half - 2)]
    *taps_of, q_own = pl.pallas_call(
        own_kernel,
        out_shape=tuple(map(on_chip_result, shapes)),
        in_specs=[vmem] * 2,
        out_specs=(vmem,) * 5,
        name="own",
    )(mine, on_chip(kernel.reshape(taps * rows, cols)))
    taps_of, q_own = list(map(on_chip, taps_of)), on_chip(q_own)
    scratch = [pltpu.VMEM(flat(n), f32) for n in (2 * halo, deep + 2 * half, halo, halo)]
    q_far, v_far = pl.pallas_call(
        far_kernel,
        out_shape=(on_chip_result(flat(HALF)),) * 2,
        in_specs=[vmem] * 7,
        out_specs=(vmem,) * 2,
        scratch_shapes=scratch,
        name="far",
    )(far, mine, q_own, *taps_of)
    v, edge, message = pl.pallas_call(
        near_kernel,
        out_shape=tuple(map(on_chip_result, (flat(deep), (deep, cols), (4, REACH * (frames + 2 * REACH), cols)))),
        in_specs=[vmem] * 9,
        out_specs=(vmem,) * 3,
        scratch_shapes=scratch,
        name="near",
    )(near, mine, q_own, *taps_of, on_chip(q_far), on_chip(v_far))
    got = lax.all_to_all(message, ("row", "col"), 0, 0, tiled=True)

    wide = rows + REACH
    out = pl.pallas_call(
        tv_kernel,
        out_shape=jax.ShapeDtypeStruct((frames * rows, cols), f32),
        in_specs=[vmem] * 3,
        out_specs=vmem,
        scratch_shapes=[
            pltpu.VMEM((wide + 1, deep + 8, cols), f32),
            pltpu.VMEM((wide, deep + 8, cols), f32),
            pltpu.VMEM((wide + 1, deep, cols), f32),
            pltpu.VMEM((wide, deep, cols), f32),
            pltpu.VMEM((deep + 8, cols), f32),
            pltpu.VMEM((deep + 8, cols), f32),
            pltpu.VMEM((4, deep, cols), f32),
        ],
        name="tv",
    )(*map(on_chip, (v, edge, got)))
    return out.reshape(frames, rows, cols)


def solution(mesh):
    in_specs = (P("tm", "row", "col"), P(None, "row", "col"))
    out_specs = P("tm", "row", "col")
    return jax.shard_map(body, mesh=mesh, in_specs=in_specs, out_specs=out_specs, check_vma=False)
```

```python
import jax
import jax.numpy as jnp
from jax import lax
from jax.experimental import pallas as pl
from jax.experimental.pallas import tpu as pltpu
from jax.sharding import PartitionSpec as P

theta = 0.1
inner_step = 1.0 / 12.0
scale = -inner_step / theta

REACH = 2
ROWS = 8
HALF = 36
COPIES = 4
BLOCK, PAIRS = 10, 6


def at(frame, count=1):
    return pl.ds(pl.multiple_of(frame * ROWS, ROWS), count * ROWS)


def far_slice_kernel(u_ref, far_ref, sems):
    size = far_ref.shape[0]
    begin = lax.rem(lax.axis_index("tm"), 2) * (u_ref.shape[0] - size)
    pieces = [(size // ROWS) * i // COPIES * ROWS for i in range(COPIES + 1)]
    copies = [
        pltpu.make_async_copy(
            u_ref.at[pl.ds(pl.multiple_of(begin + low, ROWS), high - low)], far_ref.at[low:high], sems.at[i]
        )
        for i, (low, high) in enumerate(zip(pieces, pieces[1:]))
    ]
    for copy in copies:
        copy.start()
    for copy in copies:
        copy.wait()


def near_slice_kernel(u_ref, near_ref):
    size = near_ref.shape[0]
    begin = (1 - lax.rem(lax.axis_index("tm"), 2)) * (u_ref.shape[0] - size)
    near_ref[...] = u_ref[pl.ds(pl.multiple_of(begin, ROWS), size)]


def blur(weights, field, begin, block):
    taps = weights.shape[0] // ROWS
    window = [field[at(begin + i)] for i in range(block + taps - 1)]
    acc = [None] * block
    for tap in range(taps):
        weight = weights[at(tap)]
        for i in range(block):
            term = weight * window[i + tap]
            acc[i] = term if tap == 0 else acc[i] + term
    return acc


def blur_pairs(weights, sums, field, begin, shape, pairs, finish):
    less, more = shape
    taps = weights.shape[0] // ROWS
    half = taps // 2
    count = pairs + half
    for t in range(count):
        low, high = field[at(begin + 2 * t)], field[at(begin + 2 * t + 1)]
        less[at(t)] = low - high
        if t + 1 < count:
            more[at(t)] = field[at(begin + 2 * t + 2)] - high

    def step(number, carry):
        base = number * PAIRS
        first, shared, last = [None] * PAIRS, [None] * PAIRS, [None] * PAIRS
        for k in range(half + 1):
            even, both = weights[at(2 * k)], sums[at(k)]
            odd = weights[at(2 * k + 1)] if k < half else None
            for i in range(PAIRS):
                term = even * less[at(base + i + k)]
                first[i] = first[i] + term if k else term
                term = both * field[at(begin + 2 * (base + i + k) + 1)]
                shared[i] = shared[i] + term if k else term
                if k < half:
                    term = odd * more[at(base + i + k)]
                    last[i] = last[i] + term if k else term
        for i in range(PAIRS):
            finish(2 * (base + i), first[i] + shared[i])
            finish(2 * (base + i) + 1, last[i] + shared[i])
        return carry

    lax.fori_loop(0, pairs // PAIRS, step, 0)


def own_kernel(u_ref, kernel_ref, fwd, adj, fwd_sums, adj_sums, q_ref):
    taps = kernel_ref.shape[0] // ROWS
    half = taps // 2
    total = kernel_ref[at(0)]
    for tap in range(1, taps):
        total = total + kernel_ref[at(tap)]
    inverse = 1.0 / total
    for tap in range(taps):
        share = kernel_ref[at(tap)] * inverse
        adj[at(taps - 1 - tap)] = share
        fwd[at(tap)] = (share - 1.0 if tap == half else share) * (1.0 / 3.0)
    for weights, sums in ((fwd, fwd_sums), (adj, adj_sums)):
        for k in range(half):
            sums[at(k)] = weights[at(2 * k)] + weights[at(2 * k + 1)]
        sums[at(half)] = weights[at(taps - 1)]

    def forward(step, carry):
        for i, value in enumerate(blur(fwd, u_ref, 1 + step * BLOCK, BLOCK)):
            q_ref[at(step * BLOCK + i)] = value
        return carry

    lax.fori_loop(0, q_ref.shape[0] // ROWS // BLOCK, forward, 0)


def half_blur(side, part_ref, u_ref, q_own, taps_of, u, q, less, more, v, v_begin):
    fwd, adj, fwd_sums, adj_sums = taps_of
    frames = u_ref.shape[0] // ROWS
    halo = part_ref.shape[0] // ROWS
    half = (halo - REACH) // 2
    u[at(side * halo, halo)] = part_ref[...]
    u[at((1 - side) * halo, halo)] = u_ref[at(side * (frames - halo), halo)]
    q[at(halo + 1, q_own.shape[0] // ROWS)] = q_own[...]

    def keep_q(i, value):
        q[at(side * frames + i)] = value

    blur_pairs(fwd, fwd_sums, u, 0, (less, more), HALF // 2, keep_q)
    tm = lax.axis_index("tm")
    nothing = jnp.zeros(((half + REACH) * ROWS, q.shape[1]), jnp.float32)

    @pl.when((tm == 0) & (side == 0))
    def _():
        q[at(0, half + REACH)] = nothing

    @pl.when((tm == lax.axis_size("tm") - 1) & (side == 1))
    def _():
        q[at(frames + half + REACH, half + REACH)] = nothing

    def keep_v(i, value):
        v[at(v_begin + i)] = u[at((1 - side) * 2 * half + i)] - value

    blur_pairs(adj, adj_sums, q, side * 2 * half, (less, more), HALF // 2, keep_v)


def far_kernel(part_ref, u_ref, q_own, fwd, adj, fwd_sums, adj_sums, q_ref, v_ref, u, q, less, more):
    side = lax.rem(lax.axis_index("tm"), 2)
    frames = u_ref.shape[0] // ROWS
    half_blur(side, part_ref, u_ref, q_own, (fwd, adj, fwd_sums, adj_sums), u, q, less, more, v_ref, 0)
    q_ref[...] = q[at(side * frames, HALF)]


def near_kernel(
    part_ref, u_ref, q_own, fwd, adj, fwd_sums, adj_sums, q_far, v_far, vflat, edge_ref, message_ref, u, q, less, more
):
    row, col = lax.axis_index("row"), lax.axis_index("col")
    side = 1 - lax.rem(lax.axis_index("tm"), 2)
    frames = u_ref.shape[0] // ROWS
    halo = part_ref.shape[0] // ROWS
    deep, cols = edge_ref.shape
    rows = vflat.shape[0] // deep
    span = frames + 2 * REACH
    q[at((1 - side) * frames, HALF)] = q_far[...]
    vflat[at((1 - side) * (span - HALF), HALF)] = v_far[...]
    taps_of = (fwd, adj, fwd_sums, adj_sums)
    half_blur(side, part_ref, u_ref, q_own, taps_of, u, q, less, more, vflat, side * (span - HALF))
    vflat[at(span, deep - span)] = jnp.zeros(((deep - span) * rows, cols), jnp.float32)

    lane = lax.broadcasted_iota(jnp.int32, (deep, cols), 1)
    edge = jnp.zeros((deep, cols), jnp.float32)
    for r in range(rows):
        plane = vflat[pl.ds(r, deep, stride=rows)]
        first = 4 * (r + 2 * row)
        moved = pltpu.roll(plane, first + 2, axis=1)
        low = first + 2 * col
        edge = jnp.where((lane >= low) & (lane < low + 2), moved, edge)
    edge_ref[...] = edge
    third = deep // 3
    packed = edge[:third] + pltpu.roll(edge[third : 2 * third], 40, axis=1) + pltpu.roll(edge[2 * third :], 80, axis=1)
    message_ref[2 * row + (1 - col), :third] = packed
    message_ref[2 * (1 - row) + (1 - col), :third] = packed
    begin = (rows - REACH) * (1 - row)
    for i in range(REACH):
        message_ref[2 * (1 - row) + col, i * span : (i + 1) * span] = vflat[pl.ds(begin + i, span, stride=rows)]


def unit(z_t, z_r, z_c):
    factor = lax.rsqrt(jnp.maximum(1.0, z_t * z_t + z_r * z_r + z_c * z_c))
    return z_t * factor, z_r * factor, z_c * factor


def unpacked(packed):
    lane = lax.broadcasted_iota(jnp.int32, packed.shape, 1)
    parts = [packed, pltpu.roll(packed, 88, axis=1), pltpu.roll(packed, 48, axis=1)]
    return jnp.concatenate([jnp.where(lane < 40, part, 0.0) for part in parts], axis=0)


def tv_kernel(v_ref, edge_ref, got_ref, out_ref, w, p_t, p_r, p_c, e_w, e_t, e_c):
    tm, row, col = lax.axis_index("tm"), lax.axis_index("row"), lax.axis_index("col")
    deep, cols = edge_ref.shape
    rows = v_ref.shape[0] // deep
    frames = out_ref.shape[0] // rows
    wide = rows + REACH
    span = frames + 2 * REACH

    lane = lax.broadcasted_iota(jnp.int32, (deep, cols), 1)
    time = lax.broadcasted_iota(jnp.int32, (deep, cols), 0)
    ends = ((tm == 0) & (time == REACH - 1)) | (
        (tm == lax.axis_size("tm") - 1) & (time == frames + REACH - 1)
    )
    keep_t = jnp.where(ends, 0.0, 1.0)
    keep_c = jnp.where((col == 1) & (lane == cols - 1), 0.0, 1.0)
    last, first = lane == cols - 1, lane == 0
    keep_r = jnp.where(lane < 4 * (wide - 1), 1.0, 0.0)
    is_right = jnp.where(col == 1, 1.0, 0.0)

    own = REACH * row
    foreign = rows * (1 - row)
    for r in range(rows):
        w[r + own, :deep] = v_ref[pl.ds(r, deep, stride=rows)] * scale
    for i in range(REACH):
        w[foreign + i, span:deep] = jnp.zeros((deep - span, cols), jnp.float32)
        w[foreign + i, :span] = got_ref[2 * (1 - row) + col, i * span : (i + 1) * span] * scale
    w[wide, :deep] = w[wide - 1, :deep]

    low = 4 * foreign
    corner = pltpu.roll(unpacked(got_ref[2 * (1 - row) + (1 - col), : deep // 3]), jnp.where(row == 0, 24, cols - 24), axis=1)
    edge = edge_ref[...] + unpacked(got_ref[2 * row + (1 - col), : deep // 3]) + jnp.where((lane >= low) & (lane < low + 8), corner, 0.0)
    edge = edge * scale
    for i in range(REACH):
        moved = pltpu.roll(w[foreign + i, :deep], 4 * (foreign + i) + 2, axis=1)
        begin = 4 * (foreign + i) + 2 * col
        edge = jnp.where((lane >= begin) & (lane < begin + 2), moved, edge)

    def edge_slopes(field):
        e_w[:deep] = field
        g_t = (e_w[1 : deep + 1] - field) * keep_t
        g_r = (pltpu.roll(field, cols - 4, axis=1) - field) * keep_r
        g_c = pltpu.roll(field, cols - 1, axis=1) - field
        return g_t, g_r, g_c

    e1 = unit(*edge_slopes(edge))
    e_t[8 : deep + 8] = e1[0]
    edge_div = e1[0] - e_t[7 : deep + 7] + e1[1] - pltpu.roll(e1[1], 4, axis=1) + e1[2] - pltpu.roll(e1[2], 1, axis=1)
    edge2 = edge_div * inner_step + edge
    slopes2 = edge_slopes(edge2)
    e2 = unit(e1[0] + slopes2[0], e1[1] + slopes2[1], e1[2] + slopes2[2])
    e_c[0] = edge
    e_c[1] = e1[2] * is_right
    e_c[2] = edge2
    e_c[3] = e2[2] * is_right

    def slopes(r, which):
        here = w[r, :deep]
        g_t = (w[r, 1 : deep + 1] - here) * keep_t
        g_r = w[r + 1, :deep] - here
        right = jnp.where(last, pltpu.roll(e_c[which], cols - 3 - 4 * r, axis=1), pltpu.roll(here, cols - 1, axis=1))
        return g_t, g_r, (right - here) * keep_c

    def store(r, p):
        p_t[r, 8 : deep + 8] = p[0]
        p_r[r + 1] = p[1]
        p_c[r] = p[2]

    def divergence(r, which):
        here = p_c[r]
        left = jnp.where(first, pltpu.roll(e_c[which], cols - 1 - 4 * r, axis=1), pltpu.roll(here, 1, axis=1))
        return p_t[r, 8 : deep + 8] - p_t[r, 7 : deep + 7] + p_r[r + 1] - p_r[r] + here - left

    p_r[0] = jnp.zeros((deep, cols), jnp.float32)

    def first_pass(r):
        store(r, unit(*slopes(r, 0)))

    def second_w(r):
        w[r, :deep] = divergence(r, 1) * inner_step + w[r, :deep]

    def second_pass(r):
        g_t, g_r, g_c = slopes(r, 2)
        store(r, unit(p_t[r, 8 : deep + 8] + g_t, p_r[r + 1] + g_r, p_c[r] + g_c))

    for r in range(wide):
        first_pass(r)
    for r in range(wide):
        second_w(r)
    w[wide, :deep] = w[wide - 1, :deep]
    for r in range(wide):
        second_pass(r)
    for r in range(rows):
        updated = v_ref[pl.ds(r, deep, stride=rows)] - theta * divergence(r + own, 3)
        p_c[r + own] = updated
        out_ref[pl.ds(r, frames, stride=rows)] = p_c[r + own, REACH : REACH + frames]


def on_chip(x):
    return pltpu.with_memory_space_constraint(x, pltpu.VMEM)


def on_chip_result(shape):
    return pltpu.VMEM(shape, jnp.float32)


def body(observed, kernel):
    frames, rows, cols = observed.shape
    taps = kernel.shape[0]
    half = taps // 2
    halo = 2 * half + REACH
    deep = -(-(frames + 2 * REACH) // 8) * 8
    count = lax.axis_size("tm")
    vmem = pl.BlockSpec(memory_space=pltpu.VMEM)
    f32 = jnp.float32

    mine = on_chip(observed.reshape(frames * rows, cols))
    far = pl.pallas_call(
        far_slice_kernel,
        out_shape=on_chip_result((halo * rows, cols)),
        in_specs=[pl.BlockSpec(memory_space=pl.ANY)],
        out_specs=vmem,
        scratch_shapes=[pltpu.SemaphoreType.DMA((COPIES,))],
        name="far_slice",
    )(observed.reshape(frames * rows, cols))
    near = pl.pallas_call(
        near_slice_kernel,
        out_shape=on_chip_result((halo * rows, cols)),
        in_specs=[vmem],
        out_specs=vmem,
        name="near_slice",
    )(mine)
    far = lax.ppermute(far, "tm", [(i, i + 1 if i % 2 else i - 1) for i in range(1, count - 1)])
    near = lax.ppermute(near, "tm", [(i, i ^ 1) for i in range(count)])
    near, far = on_chip(near), on_chip(far)

    def flat(count):
        return (count * rows, cols)

    shapes = [flat(n) for n in (taps, taps, half + 1, half + 1, frames - 2 * half - 2)]
    *taps_of, q_own = pl.pallas_call(
        own_kernel,
        out_shape=tuple(map(on_chip_result, shapes)),
        in_specs=[vmem] * 2,
        out_specs=(vmem,) * 5,
        name="own",
    )(mine, on_chip(kernel.reshape(taps * rows, cols)))
    taps_of, q_own = list(map(on_chip, taps_of)), on_chip(q_own)
    scratch = [pltpu.VMEM(flat(n), f32) for n in (2 * halo, deep + 2 * half, halo, halo)]
    q_far, v_far = pl.pallas_call(
        far_kernel,
        out_shape=(on_chip_result(flat(HALF)),) * 2,
        in_specs=[vmem] * 7,
        out_specs=(vmem,) * 2,
        scratch_shapes=scratch,
        name="far",
    )(far, mine, q_own, *taps_of)
    v, edge, message = pl.pallas_call(
        near_kernel,
        out_shape=tuple(map(on_chip_result, (flat(deep), (deep, cols), (4, REACH * (frames + 2 * REACH), cols)))),
        in_specs=[vmem] * 9,
        out_specs=(vmem,) * 3,
        scratch_shapes=scratch,
        name="near",
    )(near, mine, q_own, *taps_of, on_chip(q_far), on_chip(v_far))
    got = lax.all_to_all(message, ("row", "col"), 0, 0, tiled=True)

    wide = rows + REACH
    out = pl.pallas_call(
        tv_kernel,
        out_shape=jax.ShapeDtypeStruct((frames * rows, cols), f32),
        in_specs=[vmem] * 3,
        out_specs=vmem,
        scratch_shapes=[
            pltpu.VMEM((wide + 1, deep + 8, cols), f32),
            pltpu.VMEM((wide, deep + 8, cols), f32),
            pltpu.VMEM((wide + 1, deep, cols), f32),
            pltpu.VMEM((wide, deep, cols), f32),
            pltpu.VMEM((deep + 8, cols), f32),
            pltpu.VMEM((deep + 8, cols), f32),
            pltpu.VMEM((4, deep, cols), f32),
        ],
        name="tv",
    )(*map(on_chip, (v, edge, got)))
    return out.reshape(frames, rows, cols)


def solution(mesh):
    in_specs = (P("tm", "row", "col"), P(None, "row", "col"))
    out_specs = P("tm", "row", "col")
    return jax.shard_map(body, mesh=mesh, in_specs=in_specs, out_specs=out_specs, check_vma=False)
```

```python
import jax
import jax.numpy as jnp
from jax import lax
from jax.experimental import pallas as pl
from jax.experimental.pallas import tpu as pltpu
from jax.sharding import PartitionSpec as P

theta = 0.1
inner_step = 1.0 / 12.0
scale = -inner_step / theta

REACH = 2
ROWS = 8
HALF = 36
BLOCK, PAIRS = 10, 6


def at(frame, count=1):
    return pl.ds(pl.multiple_of(frame * ROWS, ROWS), count * ROWS)


def blur(weights, field, begin, block):
    taps = weights.shape[0] // ROWS
    window = [field[at(begin + i)] for i in range(block + taps - 1)]
    acc = [None] * block
    for tap in range(taps):
        weight = weights[at(tap)]
        for i in range(block):
            term = weight * window[i + tap]
            acc[i] = term if tap == 0 else acc[i] + term
    return acc


def blur_pairs(weights, sums, field, begin, shape, pairs, finish):
    less, more = shape
    taps = weights.shape[0] // ROWS
    half = taps // 2
    count = pairs + half
    for t in range(count):
        low, high = field[at(begin + 2 * t)], field[at(begin + 2 * t + 1)]
        less[at(t)] = low - high
        if t + 1 < count:
            more[at(t)] = field[at(begin + 2 * t + 2)] - high

    def step(number, carry):
        base = number * PAIRS
        first, shared, last = [None] * PAIRS, [None] * PAIRS, [None] * PAIRS
        for k in range(half + 1):
            even, both = weights[at(2 * k)], sums[at(k)]
            odd = weights[at(2 * k + 1)] if k < half else None
            for i in range(PAIRS):
                term = even * less[at(base + i + k)]
                first[i] = first[i] + term if k else term
                term = both * field[at(begin + 2 * (base + i + k) + 1)]
                shared[i] = shared[i] + term if k else term
                if k < half:
                    term = odd * more[at(base + i + k)]
                    last[i] = last[i] + term if k else term
        for i in range(PAIRS):
            finish(2 * (base + i), first[i] + shared[i])
            finish(2 * (base + i) + 1, last[i] + shared[i])
        return carry

    lax.fori_loop(0, pairs // PAIRS, step, 0, unroll=True)


def own_kernel(u_ref, kernel_ref, fwd, adj, fwd_sums, adj_sums, q_ref):
    taps = kernel_ref.shape[0] // ROWS
    half = taps // 2
    total = kernel_ref[at(0)]
    for tap in range(1, taps):
        total = total + kernel_ref[at(tap)]
    inverse = 1.0 / total
    for tap in range(taps):
        share = kernel_ref[at(tap)] * inverse
        adj[at(taps - 1 - tap)] = share
        fwd[at(tap)] = (share - 1.0 if tap == half else share) * (1.0 / 3.0)
    for weights, sums in ((fwd, fwd_sums), (adj, adj_sums)):
        for k in range(half):
            sums[at(k)] = weights[at(2 * k)] + weights[at(2 * k + 1)]
        sums[at(half)] = weights[at(taps - 1)]

    def forward(step, carry):
        for i, value in enumerate(blur(fwd, u_ref, 1 + step * BLOCK, BLOCK)):
            q_ref[at(step * BLOCK + i)] = value
        return carry

    lax.fori_loop(0, q_ref.shape[0] // ROWS // BLOCK, forward, 0, unroll=True)


def half_blur(side, part_ref, u_ref, q_own, taps_of, u, q, less, more, v, v_begin):
    fwd, adj, fwd_sums, adj_sums = taps_of
    frames = u_ref.shape[0] // ROWS
    halo = part_ref.shape[0] // ROWS
    half = (halo - REACH) // 2
    u[at(side * halo, halo)] = part_ref[...]
    u[at((1 - side) * halo, halo)] = u_ref[at(side * (frames - halo), halo)]
    q[at(halo + 1, q_own.shape[0] // ROWS)] = q_own[...]

    def keep_q(i, value):
        q[at(side * frames + i)] = value

    blur_pairs(fwd, fwd_sums, u, 0, (less, more), HALF // 2, keep_q)
    tm = lax.axis_index("tm")
    nothing = jnp.zeros(((half + REACH) * ROWS, q.shape[1]), jnp.float32)

    @pl.when((tm == 0) & (side == 0))
    def _():
        q[at(0, half + REACH)] = nothing

    @pl.when((tm == lax.axis_size("tm") - 1) & (side == 1))
    def _():
        q[at(frames + half + REACH, half + REACH)] = nothing

    def keep_v(i, value):
        v[at(v_begin + i)] = u[at((1 - side) * 2 * half + i)] - value

    blur_pairs(adj, adj_sums, q, side * 2 * half, (less, more), HALF // 2, keep_v)


def far_kernel(part_ref, u_ref, q_own, fwd, adj, fwd_sums, adj_sums, q_ref, v_ref, u, q, less, more):
    side = lax.rem(lax.axis_index("tm"), 2)
    frames = u_ref.shape[0] // ROWS
    half_blur(side, part_ref, u_ref, q_own, (fwd, adj, fwd_sums, adj_sums), u, q, less, more, v_ref, 0)
    q_ref[...] = q[at(side * frames, HALF)]


def near_kernel(
    part_ref, u_ref, q_own, fwd, adj, fwd_sums, adj_sums, q_far, v_far, vflat, edge_ref, message_ref, u, q, less, more
):
    row, col = lax.axis_index("row"), lax.axis_index("col")
    side = 1 - lax.rem(lax.axis_index("tm"), 2)
    frames = u_ref.shape[0] // ROWS
    halo = part_ref.shape[0] // ROWS
    deep, cols = edge_ref.shape
    rows = vflat.shape[0] // deep
    span = frames + 2 * REACH
    q[at((1 - side) * frames, HALF)] = q_far[...]
    vflat[at((1 - side) * (span - HALF), HALF)] = v_far[...]
    taps_of = (fwd, adj, fwd_sums, adj_sums)
    half_blur(side, part_ref, u_ref, q_own, taps_of, u, q, less, more, vflat, side * (span - HALF))
    vflat[at(span, deep - span)] = jnp.zeros(((deep - span) * rows, cols), jnp.float32)

    lane = lax.broadcasted_iota(jnp.int32, (deep, cols), 1)
    edge = jnp.zeros((deep, cols), jnp.float32)
    for r in range(rows):
        plane = vflat[pl.ds(r, deep, stride=rows)]
        first = 4 * (r + 2 * row)
        moved = pltpu.roll(plane, first + 2, axis=1)
        low = first + 2 * col
        edge = jnp.where((lane >= low) & (lane < low + 2), moved, edge)
    edge_ref[...] = edge
    third = deep // 3
    packed = edge[:third] + pltpu.roll(edge[third : 2 * third], 40, axis=1) + pltpu.roll(edge[2 * third :], 80, axis=1)
    message_ref[2 * row + (1 - col), :third] = packed
    message_ref[2 * (1 - row) + (1 - col), :third] = packed
    begin = (rows - REACH) * (1 - row)
    for i in range(REACH):
        message_ref[2 * (1 - row) + col, i * span : (i + 1) * span] = vflat[pl.ds(begin + i, span, stride=rows)]


def unit(z_t, z_r, z_c):
    factor = lax.rsqrt(jnp.maximum(1.0, z_t * z_t + z_r * z_r + z_c * z_c))
    return z_t * factor, z_r * factor, z_c * factor


def unpacked(packed):
    lane = lax.broadcasted_iota(jnp.int32, packed.shape, 1)
    parts = [packed, pltpu.roll(packed, 88, axis=1), pltpu.roll(packed, 48, axis=1)]
    return jnp.concatenate([jnp.where(lane < 40, part, 0.0) for part in parts], axis=0)


def tv_kernel(v_ref, edge_ref, got_ref, out_ref, w, p_t, p_r, p_c, e_w, e_t, e_c):
    tm, row, col = lax.axis_index("tm"), lax.axis_index("row"), lax.axis_index("col")
    deep, cols = edge_ref.shape
    rows = v_ref.shape[0] // deep
    frames = out_ref.shape[0] // rows
    wide = rows + REACH
    span = frames + 2 * REACH

    lane = lax.broadcasted_iota(jnp.int32, (deep, cols), 1)
    time = lax.broadcasted_iota(jnp.int32, (deep, cols), 0)
    ends = ((tm == 0) & (time == REACH - 1)) | (
        (tm == lax.axis_size("tm") - 1) & (time == frames + REACH - 1)
    )
    keep_t = jnp.where(ends, 0.0, 1.0)
    keep_c = jnp.where((col == 1) & (lane == cols - 1), 0.0, 1.0)
    last, first = lane == cols - 1, lane == 0
    keep_r = jnp.where(lane < 4 * (wide - 1), 1.0, 0.0)
    is_right = jnp.where(col == 1, 1.0, 0.0)

    own = REACH * row
    foreign = rows * (1 - row)
    for r in range(rows):
        w[r + own, :deep] = v_ref[pl.ds(r, deep, stride=rows)] * scale
    for i in range(REACH):
        w[foreign + i, span:deep] = jnp.zeros((deep - span, cols), jnp.float32)
        w[foreign + i, :span] = got_ref[2 * (1 - row) + col, i * span : (i + 1) * span] * scale
    w[wide, :deep] = w[wide - 1, :deep]

    low = 4 * foreign
    corner = pltpu.roll(unpacked(got_ref[2 * (1 - row) + (1 - col), : deep // 3]), jnp.where(row == 0, 24, cols - 24), axis=1)
    edge = edge_ref[...] + unpacked(got_ref[2 * row + (1 - col), : deep // 3]) + jnp.where((lane >= low) & (lane < low + 8), corner, 0.0)
    edge = edge * scale
    for i in range(REACH):
        moved = pltpu.roll(w[foreign + i, :deep], 4 * (foreign + i) + 2, axis=1)
        begin = 4 * (foreign + i) + 2 * col
        edge = jnp.where((lane >= begin) & (lane < begin + 2), moved, edge)

    def edge_slopes(field):
        e_w[:deep] = field
        g_t = (e_w[1 : deep + 1] - field) * keep_t
        g_r = (pltpu.roll(field, cols - 4, axis=1) - field) * keep_r
        g_c = pltpu.roll(field, cols - 1, axis=1) - field
        return g_t, g_r, g_c

    e1 = unit(*edge_slopes(edge))
    e_t[8 : deep + 8] = e1[0]
    edge_div = e1[0] - e_t[7 : deep + 7] + e1[1] - pltpu.roll(e1[1], 4, axis=1) + e1[2] - pltpu.roll(e1[2], 1, axis=1)
    edge2 = edge_div * inner_step + edge
    slopes2 = edge_slopes(edge2)
    e2 = unit(e1[0] + slopes2[0], e1[1] + slopes2[1], e1[2] + slopes2[2])
    e_c[0] = edge
    e_c[1] = e1[2] * is_right
    e_c[2] = edge2
    e_c[3] = e2[2] * is_right

    def slopes(r, which):
        here = w[r, :deep]
        g_t = (w[r, 1 : deep + 1] - here) * keep_t
        g_r = w[r + 1, :deep] - here
        right = jnp.where(last, pltpu.roll(e_c[which], cols - 3 - 4 * r, axis=1), pltpu.roll(here, cols - 1, axis=1))
        return g_t, g_r, (right - here) * keep_c

    def store(r, p):
        p_t[r, 8 : deep + 8] = p[0]
        p_r[r + 1] = p[1]
        p_c[r] = p[2]

    def divergence(r, which):
        here = p_c[r]
        left = jnp.where(first, pltpu.roll(e_c[which], cols - 1 - 4 * r, axis=1), pltpu.roll(here, 1, axis=1))
        return p_t[r, 8 : deep + 8] - p_t[r, 7 : deep + 7] + p_r[r + 1] - p_r[r] + here - left

    p_r[0] = jnp.zeros((deep, cols), jnp.float32)

    def first_pass(r):
        store(r, unit(*slopes(r, 0)))

    def second_w(r):
        w[r, :deep] = divergence(r, 1) * inner_step + w[r, :deep]

    def second_pass(r):
        g_t, g_r, g_c = slopes(r, 2)
        store(r, unit(p_t[r, 8 : deep + 8] + g_t, p_r[r + 1] + g_r, p_c[r] + g_c))

    for r in range(wide):
        first_pass(r)
    for r in range(wide):
        second_w(r)
    w[wide, :deep] = w[wide - 1, :deep]
    for r in range(wide):
        second_pass(r)
    for r in range(rows):
        updated = v_ref[pl.ds(r, deep, stride=rows)] - theta * divergence(r + own, 3)
        p_c[r + own] = updated
        out_ref[pl.ds(r, frames, stride=rows)] = p_c[r + own, REACH : REACH + frames]


def on_chip(x):
    return pltpu.with_memory_space_constraint(x, pltpu.VMEM)


def on_chip_result(shape):
    return pltpu.VMEM(shape, jnp.float32)


def body(observed, kernel):
    frames, rows, cols = observed.shape
    taps = kernel.shape[0]
    half = taps // 2
    halo = 2 * half + REACH
    deep = -(-(frames + 2 * REACH) // 8) * 8
    count = lax.axis_size("tm")
    odd = lax.axis_index("tm") % 2
    vmem = pl.BlockSpec(memory_space=pltpu.VMEM)
    f32 = jnp.float32

    near = lax.dynamic_slice_in_dim(observed, (1 - odd) * (frames - halo), halo, axis=0).reshape(halo * rows, cols)
    far = lax.dynamic_slice_in_dim(observed, odd * (frames - halo), halo, axis=0).reshape(halo * rows, cols)
    far = lax.ppermute(far, "tm", [(i, i + 1 if i % 2 else i - 1) for i in range(1, count - 1)])
    near = lax.ppermute(near, "tm", [(i, i ^ 1) for i in range(count)])
    near, far = on_chip(near), on_chip(far)
    mine = on_chip(observed.reshape(frames * rows, cols))

    def flat(count):
        return (count * rows, cols)

    shapes = [flat(n) for n in (taps, taps, half + 1, half + 1, frames - 2 * half - 2)]
    *taps_of, q_own = pl.pallas_call(
        own_kernel,
        out_shape=tuple(map(on_chip_result, shapes)),
        in_specs=[vmem] * 2,
        out_specs=(vmem,) * 5,
        name="own",
    )(mine, on_chip(kernel.reshape(taps * rows, cols)))
    taps_of, q_own = list(map(on_chip, taps_of)), on_chip(q_own)
    scratch = [pltpu.VMEM(flat(n), f32) for n in (2 * halo, deep + 2 * half, halo, halo)]
    q_far, v_far = pl.pallas_call(
        far_kernel,
        out_shape=(on_chip_result(flat(HALF)),) * 2,
        in_specs=[vmem] * 7,
        out_specs=(vmem,) * 2,
        scratch_shapes=scratch,
        name="far",
    )(far, mine, q_own, *taps_of)
    v, edge, message = pl.pallas_call(
        near_kernel,
        out_shape=tuple(map(on_chip_result, (flat(deep), (deep, cols), (4, REACH * (frames + 2 * REACH), cols)))),
        in_specs=[vmem] * 9,
        out_specs=(vmem,) * 3,
        scratch_shapes=scratch,
        name="near",
    )(near, mine, q_own, *taps_of, on_chip(q_far), on_chip(v_far))
    got = lax.all_to_all(message, ("row", "col"), 0, 0, tiled=True)

    wide = rows + REACH
    out = pl.pallas_call(
        tv_kernel,
        out_shape=jax.ShapeDtypeStruct((frames * rows, cols), f32),
        in_specs=[vmem] * 3,
        out_specs=vmem,
        scratch_shapes=[
            pltpu.VMEM((wide + 1, deep + 8, cols), f32),
            pltpu.VMEM((wide, deep + 8, cols), f32),
            pltpu.VMEM((wide + 1, deep, cols), f32),
            pltpu.VMEM((wide, deep, cols), f32),
            pltpu.VMEM((deep + 8, cols), f32),
            pltpu.VMEM((deep + 8, cols), f32),
            pltpu.VMEM((4, deep, cols), f32),
        ],
        name="tv",
    )(*map(on_chip, (v, edge, got)))
    return out.reshape(frames, rows, cols)


def solution(mesh):
    in_specs = (P("tm", "row", "col"), P(None, "row", "col"))
    out_specs = P("tm", "row", "col")
    return jax.shard_map(body, mesh=mesh, in_specs=in_specs, out_specs=out_specs, check_vma=False)
```

```python
import jax
import jax.numpy as jnp
from jax import lax
from jax.experimental import pallas as pl
from jax.experimental.pallas import tpu as pltpu
from jax.sharding import PartitionSpec as P

theta = 0.1
inner_step = 1.0 / 12.0
scale = -inner_step / theta

REACH = 2
ROWS = 8
HALF = 36
COPIES = 4
BLOCK, PAIRS = 10, 6


def at(frame, count=1):
    return pl.ds(pl.multiple_of(frame * ROWS, ROWS), count * ROWS)


def far_slice_kernel(u_ref, far_ref, sems):
    size = far_ref.shape[0]
    begin = lax.rem(lax.axis_index("tm"), 2) * (u_ref.shape[0] - size)
    pieces = [(size // ROWS) * i // COPIES * ROWS for i in range(COPIES + 1)]
    copies = [
        pltpu.make_async_copy(
            u_ref.at[pl.ds(pl.multiple_of(begin + low, ROWS), high - low)], far_ref.at[low:high], sems.at[i]
        )
        for i, (low, high) in enumerate(zip(pieces, pieces[1:]))
    ]
    for copy in copies:
        copy.start()
    for copy in copies:
        copy.wait()


def near_slice_kernel(u_ref, near_ref):
    size = near_ref.shape[0]
    begin = (1 - lax.rem(lax.axis_index("tm"), 2)) * (u_ref.shape[0] - size)
    near_ref[...] = u_ref[pl.ds(pl.multiple_of(begin, ROWS), size)]


def blur(weights, field, begin, block):
    taps = weights.shape[0] // ROWS
    window = [field[at(begin + i)] for i in range(block + taps - 1)]
    acc = [None] * block
    for tap in range(taps):
        weight = weights[at(tap)]
        for i in range(block):
            term = weight * window[i + tap]
            acc[i] = term if tap == 0 else acc[i] + term
    return acc


def blur_pairs(weights, sums, field, begin, shape, pairs, finish):
    less, more = shape
    taps = weights.shape[0] // ROWS
    half = taps // 2
    count = pairs + half
    for t in range(count):
        low, high = field[at(begin + 2 * t)], field[at(begin + 2 * t + 1)]
        less[at(t)] = low - high
        if t + 1 < count:
            more[at(t)] = field[at(begin + 2 * t + 2)] - high

    def step(number, carry):
        base = number * PAIRS
        first, shared, last = [None] * PAIRS, [None] * PAIRS, [None] * PAIRS
        for k in range(half + 1):
            even, both = weights[at(2 * k)], sums[at(k)]
            odd = weights[at(2 * k + 1)] if k < half else None
            for i in range(PAIRS):
                term = even * less[at(base + i + k)]
                first[i] = first[i] + term if k else term
                term = both * field[at(begin + 2 * (base + i + k) + 1)]
                shared[i] = shared[i] + term if k else term
                if k < half:
                    term = odd * more[at(base + i + k)]
                    last[i] = last[i] + term if k else term
        for i in range(PAIRS):
            finish(2 * (base + i), first[i] + shared[i])
            finish(2 * (base + i) + 1, last[i] + shared[i])
        return carry

    lax.fori_loop(0, pairs // PAIRS, step, 0, unroll=True)


def own_kernel(u_ref, kernel_ref, fwd, adj, fwd_sums, adj_sums, q_ref):
    taps = kernel_ref.shape[0] // ROWS
    half = taps // 2
    total = kernel_ref[at(0)]
    for tap in range(1, taps):
        total = total + kernel_ref[at(tap)]
    inverse = 1.0 / total
    for tap in range(taps):
        share = kernel_ref[at(tap)] * inverse
        adj[at(taps - 1 - tap)] = share
        fwd[at(tap)] = (share - 1.0 if tap == half else share) * (1.0 / 3.0)
    for weights, sums in ((fwd, fwd_sums), (adj, adj_sums)):
        for k in range(half):
            sums[at(k)] = weights[at(2 * k)] + weights[at(2 * k + 1)]
        sums[at(half)] = weights[at(taps - 1)]

    def forward(step, carry):
        for i, value in enumerate(blur(fwd, u_ref, 1 + step * BLOCK, BLOCK)):
            q_ref[at(step * BLOCK + i)] = value
        return carry

    lax.fori_loop(0, q_ref.shape[0] // ROWS // BLOCK, forward, 0, unroll=True)


def half_blur(side, part_ref, u_ref, q_own, taps_of, u, q, less, more, v, v_begin):
    fwd, adj, fwd_sums, adj_sums = taps_of
    frames = u_ref.shape[0] // ROWS
    halo = part_ref.shape[0] // ROWS
    half = (halo - REACH) // 2
    u[at(side * halo, halo)] = part_ref[...]
    u[at((1 - side) * halo, halo)] = u_ref[at(side * (frames - halo), halo)]
    q[at(halo + 1, q_own.shape[0] // ROWS)] = q_own[...]

    def keep_q(i, value):
        q[at(side * frames + i)] = value

    blur_pairs(fwd, fwd_sums, u, 0, (less, more), HALF // 2, keep_q)
    tm = lax.axis_index("tm")
    nothing = jnp.zeros(((half + REACH) * ROWS, q.shape[1]), jnp.float32)

    @pl.when((tm == 0) & (side == 0))
    def _():
        q[at(0, half + REACH)] = nothing

    @pl.when((tm == lax.axis_size("tm") - 1) & (side == 1))
    def _():
        q[at(frames + half + REACH, half + REACH)] = nothing

    def keep_v(i, value):
        v[at(v_begin + i)] = u[at((1 - side) * 2 * half + i)] - value

    blur_pairs(adj, adj_sums, q, side * 2 * half, (less, more), HALF // 2, keep_v)


def far_kernel(part_ref, u_ref, q_own, fwd, adj, fwd_sums, adj_sums, q_ref, v_ref, u, q, less, more):
    side = lax.rem(lax.axis_index("tm"), 2)
    frames = u_ref.shape[0] // ROWS
    half_blur(side, part_ref, u_ref, q_own, (fwd, adj, fwd_sums, adj_sums), u, q, less, more, v_ref, 0)
    q_ref[...] = q[at(side * frames, HALF)]


def near_kernel(
    part_ref, u_ref, q_own, fwd, adj, fwd_sums, adj_sums, q_far, v_far, vflat, edge_ref, message_ref, u, q, less, more
):
    row, col = lax.axis_index("row"), lax.axis_index("col")
    side = 1 - lax.rem(lax.axis_index("tm"), 2)
    frames = u_ref.shape[0] // ROWS
    halo = part_ref.shape[0] // ROWS
    deep, cols = edge_ref.shape
    rows = vflat.shape[0] // deep
    span = frames + 2 * REACH
    q[at((1 - side) * frames, HALF)] = q_far[...]
    vflat[at((1 - side) * (span - HALF), HALF)] = v_far[...]
    taps_of = (fwd, adj, fwd_sums, adj_sums)
    half_blur(side, part_ref, u_ref, q_own, taps_of, u, q, less, more, vflat, side * (span - HALF))
    vflat[at(span, deep - span)] = jnp.zeros(((deep - span) * rows, cols), jnp.float32)

    lane = lax.broadcasted_iota(jnp.int32, (deep, cols), 1)
    edge = jnp.zeros((deep, cols), jnp.float32)
    for r in range(rows):
        plane = vflat[pl.ds(r, deep, stride=rows)]
        first = 4 * (r + 2 * row)
        moved = pltpu.roll(plane, first + 2, axis=1)
        low = first + 2 * col
        edge = jnp.where((lane >= low) & (lane < low + 2), moved, edge)
    edge_ref[...] = edge
    third = deep // 3
    packed = edge[:third] + pltpu.roll(edge[third : 2 * third], 40, axis=1) + pltpu.roll(edge[2 * third :], 80, axis=1)
    message_ref[2 * row + (1 - col), :third] = packed
    message_ref[2 * (1 - row) + (1 - col), :third] = packed
    begin = (rows - REACH) * (1 - row)
    for i in range(REACH):
        message_ref[2 * (1 - row) + col, i * span : (i + 1) * span] = vflat[pl.ds(begin + i, span, stride=rows)]


def unit(z_t, z_r, z_c):
    factor = lax.rsqrt(jnp.maximum(1.0, z_t * z_t + z_r * z_r + z_c * z_c))
    return z_t * factor, z_r * factor, z_c * factor


def unpacked(packed):
    lane = lax.broadcasted_iota(jnp.int32, packed.shape, 1)
    parts = [packed, pltpu.roll(packed, 88, axis=1), pltpu.roll(packed, 48, axis=1)]
    return jnp.concatenate([jnp.where(lane < 40, part, 0.0) for part in parts], axis=0)


def tv_kernel(v_ref, edge_ref, got_ref, out_ref, w, p_t, p_r, p_c, e_w, e_t, e_c):
    tm, row, col = lax.axis_index("tm"), lax.axis_index("row"), lax.axis_index("col")
    deep, cols = edge_ref.shape
    rows = v_ref.shape[0] // deep
    frames = out_ref.shape[0] // rows
    wide = rows + REACH
    span = frames + 2 * REACH

    lane = lax.broadcasted_iota(jnp.int32, (deep, cols), 1)
    time = lax.broadcasted_iota(jnp.int32, (deep, cols), 0)
    ends = ((tm == 0) & (time == REACH - 1)) | (
        (tm == lax.axis_size("tm") - 1) & (time == frames + REACH - 1)
    )
    keep_t = jnp.where(ends, 0.0, 1.0)
    keep_c = jnp.where((col == 1) & (lane == cols - 1), 0.0, 1.0)
    last, first = lane == cols - 1, lane == 0
    keep_r = jnp.where(lane < 4 * (wide - 1), 1.0, 0.0)
    is_right = jnp.where(col == 1, 1.0, 0.0)

    own = REACH * row
    foreign = rows * (1 - row)
    for r in range(rows):
        w[r + own, :deep] = v_ref[pl.ds(r, deep, stride=rows)] * scale
    for i in range(REACH):
        w[foreign + i, span:deep] = jnp.zeros((deep - span, cols), jnp.float32)
        w[foreign + i, :span] = got_ref[2 * (1 - row) + col, i * span : (i + 1) * span] * scale
    w[wide, :deep] = w[wide - 1, :deep]

    low = 4 * foreign
    corner = pltpu.roll(unpacked(got_ref[2 * (1 - row) + (1 - col), : deep // 3]), jnp.where(row == 0, 24, cols - 24), axis=1)
    edge = edge_ref[...] + unpacked(got_ref[2 * row + (1 - col), : deep // 3]) + jnp.where((lane >= low) & (lane < low + 8), corner, 0.0)
    edge = edge * scale
    for i in range(REACH):
        moved = pltpu.roll(w[foreign + i, :deep], 4 * (foreign + i) + 2, axis=1)
        begin = 4 * (foreign + i) + 2 * col
        edge = jnp.where((lane >= begin) & (lane < begin + 2), moved, edge)

    def edge_slopes(field):
        e_w[:deep] = field
        g_t = (e_w[1 : deep + 1] - field) * keep_t
        g_r = (pltpu.roll(field, cols - 4, axis=1) - field) * keep_r
        g_c = pltpu.roll(field, cols - 1, axis=1) - field
        return g_t, g_r, g_c

    e1 = unit(*edge_slopes(edge))
    e_t[8 : deep + 8] = e1[0]
    edge_div = e1[0] - e_t[7 : deep + 7] + e1[1] - pltpu.roll(e1[1], 4, axis=1) + e1[2] - pltpu.roll(e1[2], 1, axis=1)
    edge2 = edge_div * inner_step + edge
    slopes2 = edge_slopes(edge2)
    e2 = unit(e1[0] + slopes2[0], e1[1] + slopes2[1], e1[2] + slopes2[2])
    e_c[0] = edge
    e_c[1] = e1[2] * is_right
    e_c[2] = edge2
    e_c[3] = e2[2] * is_right

    def slopes(r, which):
        here = w[r, :deep]
        g_t = (w[r, 1 : deep + 1] - here) * keep_t
        g_r = w[r + 1, :deep] - here
        right = jnp.where(last, pltpu.roll(e_c[which], cols - 3 - 4 * r, axis=1), pltpu.roll(here, cols - 1, axis=1))
        return g_t, g_r, (right - here) * keep_c

    def store(r, p):
        p_t[r, 8 : deep + 8] = p[0]
        p_r[r + 1] = p[1]
        p_c[r] = p[2]

    def divergence(r, which):
        here = p_c[r]
        left = jnp.where(first, pltpu.roll(e_c[which], cols - 1 - 4 * r, axis=1), pltpu.roll(here, 1, axis=1))
        return p_t[r, 8 : deep + 8] - p_t[r, 7 : deep + 7] + p_r[r + 1] - p_r[r] + here - left

    p_r[0] = jnp.zeros((deep, cols), jnp.float32)

    def first_pass(r):
        store(r, unit(*slopes(r, 0)))

    def second_w(r):
        w[r, :deep] = divergence(r, 1) * inner_step + w[r, :deep]

    def second_pass(r):
        g_t, g_r, g_c = slopes(r, 2)
        store(r, unit(p_t[r, 8 : deep + 8] + g_t, p_r[r + 1] + g_r, p_c[r] + g_c))

    for r in range(wide):
        first_pass(r)
    for r in range(wide):
        second_w(r)
    w[wide, :deep] = w[wide - 1, :deep]
    for r in range(wide):
        second_pass(r)
    for r in range(rows):
        updated = v_ref[pl.ds(r, deep, stride=rows)] - theta * divergence(r + own, 3)
        p_c[r + own] = updated
        out_ref[pl.ds(r, frames, stride=rows)] = p_c[r + own, REACH : REACH + frames]


def on_chip(x):
    return pltpu.with_memory_space_constraint(x, pltpu.VMEM)


def on_chip_result(shape):
    return pltpu.VMEM(shape, jnp.float32)


def body(observed, kernel):
    frames, rows, cols = observed.shape
    taps = kernel.shape[0]
    half = taps // 2
    halo = 2 * half + REACH
    deep = -(-(frames + 2 * REACH) // 8) * 8
    count = lax.axis_size("tm")
    vmem = pl.BlockSpec(memory_space=pltpu.VMEM)
    f32 = jnp.float32

    mine = on_chip(observed.reshape(frames * rows, cols))
    far = pl.pallas_call(
        far_slice_kernel,
        out_shape=on_chip_result((halo * rows, cols)),
        in_specs=[pl.BlockSpec(memory_space=pl.ANY)],
        out_specs=vmem,
        scratch_shapes=[pltpu.SemaphoreType.DMA((COPIES,))],
        name="far_slice",
    )(observed.reshape(frames * rows, cols))
    near = pl.pallas_call(
        near_slice_kernel,
        out_shape=on_chip_result((halo * rows, cols)),
        in_specs=[vmem],
        out_specs=vmem,
        name="near_slice",
    )(mine)
    far = lax.ppermute(far, "tm", [(i, i + 1 if i % 2 else i - 1) for i in range(1, count - 1)])
    near = lax.ppermute(near, "tm", [(i, i ^ 1) for i in range(count)])
    near, far = on_chip(near), on_chip(far)

    def flat(count):
        return (count * rows, cols)

    shapes = [flat(n) for n in (taps, taps, half + 1, half + 1, frames - 2 * half - 2)]
    *taps_of, q_own = pl.pallas_call(
        own_kernel,
        out_shape=tuple(map(on_chip_result, shapes)),
        in_specs=[vmem] * 2,
        out_specs=(vmem,) * 5,
        name="own",
    )(mine, on_chip(kernel.reshape(taps * rows, cols)))
    taps_of, q_own = list(map(on_chip, taps_of)), on_chip(q_own)
    scratch = [pltpu.VMEM(flat(n), f32) for n in (2 * halo, deep + 2 * half, halo, halo)]
    q_far, v_far = pl.pallas_call(
        far_kernel,
        out_shape=(on_chip_result(flat(HALF)),) * 2,
        in_specs=[vmem] * 7,
        out_specs=(vmem,) * 2,
        scratch_shapes=scratch,
        name="far",
    )(far, mine, q_own, *taps_of)
    v, edge, message = pl.pallas_call(
        near_kernel,
        out_shape=tuple(map(on_chip_result, (flat(deep), (deep, cols), (4, REACH * (frames + 2 * REACH), cols)))),
        in_specs=[vmem] * 9,
        out_specs=(vmem,) * 3,
        scratch_shapes=scratch,
        name="near",
    )(near, mine, q_own, *taps_of, on_chip(q_far), on_chip(v_far))
    got = lax.all_to_all(message, ("row", "col"), 0, 0, tiled=True)

    wide = rows + REACH
    out = pl.pallas_call(
        tv_kernel,
        out_shape=jax.ShapeDtypeStruct((frames * rows, cols), f32),
        in_specs=[vmem] * 3,
        out_specs=vmem,
        scratch_shapes=[
            pltpu.VMEM((wide + 1, deep + 8, cols), f32),
            pltpu.VMEM((wide, deep + 8, cols), f32),
            pltpu.VMEM((wide + 1, deep, cols), f32),
            pltpu.VMEM((wide, deep, cols), f32),
            pltpu.VMEM((deep + 8, cols), f32),
            pltpu.VMEM((deep + 8, cols), f32),
            pltpu.VMEM((4, deep, cols), f32),
        ],
        name="tv",
    )(*map(on_chip, (v, edge, got)))
    return out.reshape(frames, rows, cols)


def solution(mesh):
    in_specs = (P("tm", "row", "col"), P(None, "row", "col"))
    out_specs = P("tm", "row", "col")
    return jax.shard_map(body, mesh=mesh, in_specs=in_specs, out_specs=out_specs, check_vma=False)
```

```python
import jax
import jax.numpy as jnp
from jax import lax
from jax.experimental import pallas as pl
from jax.experimental.pallas import tpu as pltpu
from jax.sharding import PartitionSpec as P

theta = 0.1
inner_step = 1.0 / 12.0
scale = -inner_step / theta

REACH = 2
ROWS = 8
HALF = 36
COPIES = 4
BLOCK, PAIRS = 10, 9


def at(frame, count=1):
    return pl.ds(pl.multiple_of(frame * ROWS, ROWS), count * ROWS)


def far_slice_kernel(u_ref, far_ref, sems):
    size = far_ref.shape[0]
    begin = lax.rem(lax.axis_index("tm"), 2) * (u_ref.shape[0] - size)
    pieces = [(size // ROWS) * i // COPIES * ROWS for i in range(COPIES + 1)]
    copies = [
        pltpu.make_async_copy(
            u_ref.at[pl.ds(pl.multiple_of(begin + low, ROWS), high - low)], far_ref.at[low:high], sems.at[i]
        )
        for i, (low, high) in enumerate(zip(pieces, pieces[1:]))
    ]
    for copy in copies:
        copy.start()
    for copy in copies:
        copy.wait()


def near_slice_kernel(u_ref, near_ref):
    size = near_ref.shape[0]
    begin = (1 - lax.rem(lax.axis_index("tm"), 2)) * (u_ref.shape[0] - size)
    near_ref[...] = u_ref[pl.ds(pl.multiple_of(begin, ROWS), size)]


def blur(weights, field, begin, block):
    taps = weights.shape[0] // ROWS
    window = [field[at(begin + i)] for i in range(block + taps - 1)]
    acc = [None] * block
    for tap in range(taps):
        weight = weights[at(tap)]
        for i in range(block):
            term = weight * window[i + tap]
            acc[i] = term if tap == 0 else acc[i] + term
    return acc


def blur_pairs(weights, sums, field, begin, shape, pairs, finish):
    less, more = shape
    taps = weights.shape[0] // ROWS
    half = taps // 2
    count = pairs + half
    for t in range(count):
        low, high = field[at(begin + 2 * t)], field[at(begin + 2 * t + 1)]
        less[at(t)] = low - high
        if t + 1 < count:
            more[at(t)] = field[at(begin + 2 * t + 2)] - high

    def step(number, carry):
        base = number * PAIRS
        first, shared, last = [None] * PAIRS, [None] * PAIRS, [None] * PAIRS
        for k in range(half + 1):
            even, both = weights[at(2 * k)], sums[at(k)]
            odd = weights[at(2 * k + 1)] if k < half else None
            for i in range(PAIRS):
                term = even * less[at(base + i + k)]
                first[i] = first[i] + term if k else term
                term = both * field[at(begin + 2 * (base + i + k) + 1)]
                shared[i] = shared[i] + term if k else term
                if k < half:
                    term = odd * more[at(base + i + k)]
                    last[i] = last[i] + term if k else term
        for i in range(PAIRS):
            finish(2 * (base + i), first[i] + shared[i])
            finish(2 * (base + i) + 1, last[i] + shared[i])
        return carry

    lax.fori_loop(0, pairs // PAIRS, step, 0, unroll=True)


def own_kernel(u_ref, kernel_ref, fwd, adj, fwd_sums, adj_sums, q_ref):
    taps = kernel_ref.shape[0] // ROWS
    half = taps // 2
    total = kernel_ref[at(0)]
    for tap in range(1, taps):
        total = total + kernel_ref[at(tap)]
    inverse = 1.0 / total
    for tap in range(taps):
        share = kernel_ref[at(tap)] * inverse
        adj[at(taps - 1 - tap)] = share
        fwd[at(tap)] = (share - 1.0 if tap == half else share) * (1.0 / 3.0)
    for weights, sums in ((fwd, fwd_sums), (adj, adj_sums)):
        for k in range(half):
            sums[at(k)] = weights[at(2 * k)] + weights[at(2 * k + 1)]
        sums[at(half)] = weights[at(taps - 1)]

    def forward(step, carry):
        for i, value in enumerate(blur(fwd, u_ref, 1 + step * BLOCK, BLOCK)):
            q_ref[at(step * BLOCK + i)] = value
        return carry

    lax.fori_loop(0, q_ref.shape[0] // ROWS // BLOCK, forward, 0, unroll=True)


def half_blur(side, part_ref, u_ref, q_own, taps_of, u, q, less, more, v, v_begin):
    fwd, adj, fwd_sums, adj_sums = taps_of
    frames = u_ref.shape[0] // ROWS
    halo = part_ref.shape[0] // ROWS
    half = (halo - REACH) // 2
    u[at(side * halo, halo)] = part_ref[...]
    u[at((1 - side) * halo, halo)] = u_ref[at(side * (frames - halo), halo)]
    q[at(halo + 1, q_own.shape[0] // ROWS)] = q_own[...]

    def keep_q(i, value):
        q[at(side * frames + i)] = value

    blur_pairs(fwd, fwd_sums, u, 0, (less, more), HALF // 2, keep_q)
    tm = lax.axis_index("tm")
    nothing = jnp.zeros(((half + REACH) * ROWS, q.shape[1]), jnp.float32)

    @pl.when((tm == 0) & (side == 0))
    def _():
        q[at(0, half + REACH)] = nothing

    @pl.when((tm == lax.axis_size("tm") - 1) & (side == 1))
    def _():
        q[at(frames + half + REACH, half + REACH)] = nothing

    def keep_v(i, value):
        v[at(v_begin + i)] = u[at((1 - side) * 2 * half + i)] - value

    blur_pairs(adj, adj_sums, q, side * 2 * half, (less, more), HALF // 2, keep_v)


def far_kernel(part_ref, u_ref, q_own, fwd, adj, fwd_sums, adj_sums, q_ref, v_ref, u, q, less, more):
    side = lax.rem(lax.axis_index("tm"), 2)
    frames = u_ref.shape[0] // ROWS
    half_blur(side, part_ref, u_ref, q_own, (fwd, adj, fwd_sums, adj_sums), u, q, less, more, v_ref, 0)
    q_ref[...] = q[at(side * frames, HALF)]


def near_kernel(
    part_ref, u_ref, q_own, fwd, adj, fwd_sums, adj_sums, q_far, v_far, vflat, edge_ref, message_ref, u, q, less, more
):
    row, col = lax.axis_index("row"), lax.axis_index("col")
    side = 1 - lax.rem(lax.axis_index("tm"), 2)
    frames = u_ref.shape[0] // ROWS
    halo = part_ref.shape[0] // ROWS
    deep, cols = edge_ref.shape
    rows = vflat.shape[0] // deep
    span = frames + 2 * REACH
    q[at((1 - side) * frames, HALF)] = q_far[...]
    vflat[at((1 - side) * (span - HALF), HALF)] = v_far[...]
    taps_of = (fwd, adj, fwd_sums, adj_sums)
    half_blur(side, part_ref, u_ref, q_own, taps_of, u, q, less, more, vflat, side * (span - HALF))
    vflat[at(span, deep - span)] = jnp.zeros(((deep - span) * rows, cols), jnp.float32)

    lane = lax.broadcasted_iota(jnp.int32, (deep, cols), 1)
    edge = jnp.zeros((deep, cols), jnp.float32)
    for r in range(rows):
        plane = vflat[pl.ds(r, deep, stride=rows)]
        first = 4 * (r + 2 * row)
        moved = pltpu.roll(plane, first + 2, axis=1)
        low = first + 2 * col
        edge = jnp.where((lane >= low) & (lane < low + 2), moved, edge)
    edge_ref[...] = edge
    third = deep // 3
    packed = edge[:third] + pltpu.roll(edge[third : 2 * third], 40, axis=1) + pltpu.roll(edge[2 * third :], 80, axis=1)
    message_ref[2 * row + (1 - col), :third] = packed
    message_ref[2 * (1 - row) + (1 - col), :third] = packed
    begin = (rows - REACH) * (1 - row)
    for i in range(REACH):
        message_ref[2 * (1 - row) + col, i * span : (i + 1) * span] = vflat[pl.ds(begin + i, span, stride=rows)]


def unit(z_t, z_r, z_c):
    factor = lax.rsqrt(jnp.maximum(1.0, z_t * z_t + z_r * z_r + z_c * z_c))
    return z_t * factor, z_r * factor, z_c * factor


def unpacked(packed):
    lane = lax.broadcasted_iota(jnp.int32, packed.shape, 1)
    parts = [packed, pltpu.roll(packed, 88, axis=1), pltpu.roll(packed, 48, axis=1)]
    return jnp.concatenate([jnp.where(lane < 40, part, 0.0) for part in parts], axis=0)


def tv_kernel(v_ref, edge_ref, got_ref, out_ref, w, p_t, p_r, p_c, e_w, e_t, e_c):
    tm, row, col = lax.axis_index("tm"), lax.axis_index("row"), lax.axis_index("col")
    deep, cols = edge_ref.shape
    rows = v_ref.shape[0] // deep
    frames = out_ref.shape[0] // rows
    wide = rows + REACH
    span = frames + 2 * REACH

    lane = lax.broadcasted_iota(jnp.int32, (deep, cols), 1)
    time = lax.broadcasted_iota(jnp.int32, (deep, cols), 0)
    ends = ((tm == 0) & (time == REACH - 1)) | (
        (tm == lax.axis_size("tm") - 1) & (time == frames + REACH - 1)
    )
    keep_t = jnp.where(ends, 0.0, 1.0)
    keep_c = jnp.where((col == 1) & (lane == cols - 1), 0.0, 1.0)
    last, first = lane == cols - 1, lane == 0
    keep_r = jnp.where(lane < 4 * (wide - 1), 1.0, 0.0)
    is_right = jnp.where(col == 1, 1.0, 0.0)

    own = REACH * row
    foreign = rows * (1 - row)
    for r in range(rows):
        w[r + own, :deep] = v_ref[pl.ds(r, deep, stride=rows)] * scale
    for i in range(REACH):
        w[foreign + i, span:deep] = jnp.zeros((deep - span, cols), jnp.float32)
        w[foreign + i, :span] = got_ref[2 * (1 - row) + col, i * span : (i + 1) * span] * scale
    w[wide, :deep] = w[wide - 1, :deep]

    low = 4 * foreign
    corner = pltpu.roll(unpacked(got_ref[2 * (1 - row) + (1 - col), : deep // 3]), jnp.where(row == 0, 24, cols - 24), axis=1)
    edge = edge_ref[...] + unpacked(got_ref[2 * row + (1 - col), : deep // 3]) + jnp.where((lane >= low) & (lane < low + 8), corner, 0.0)
    edge = edge * scale
    for i in range(REACH):
        moved = pltpu.roll(w[foreign + i, :deep], 4 * (foreign + i) + 2, axis=1)
        begin = 4 * (foreign + i) + 2 * col
        edge = jnp.where((lane >= begin) & (lane < begin + 2), moved, edge)

    def edge_slopes(field):
        e_w[:deep] = field
        g_t = (e_w[1 : deep + 1] - field) * keep_t
        g_r = (pltpu.roll(field, cols - 4, axis=1) - field) * keep_r
        g_c = pltpu.roll(field, cols - 1, axis=1) - field
        return g_t, g_r, g_c

    e1 = unit(*edge_slopes(edge))
    e_t[8 : deep + 8] = e1[0]
    edge_div = e1[0] - e_t[7 : deep + 7] + e1[1] - pltpu.roll(e1[1], 4, axis=1) + e1[2] - pltpu.roll(e1[2], 1, axis=1)
    edge2 = edge_div * inner_step + edge
    slopes2 = edge_slopes(edge2)
    e2 = unit(e1[0] + slopes2[0], e1[1] + slopes2[1], e1[2] + slopes2[2])
    e_c[0] = edge
    e_c[1] = e1[2] * is_right
    e_c[2] = edge2
    e_c[3] = e2[2] * is_right

    def slopes(r, which):
        here = w[r, :deep]
        g_t = (w[r, 1 : deep + 1] - here) * keep_t
        g_r = w[r + 1, :deep] - here
        right = jnp.where(last, pltpu.roll(e_c[which], cols - 3 - 4 * r, axis=1), pltpu.roll(here, cols - 1, axis=1))
        return g_t, g_r, (right - here) * keep_c

    def store(r, p):
        p_t[r, 8 : deep + 8] = p[0]
        p_r[r + 1] = p[1]
        p_c[r] = p[2]

    def divergence(r, which):
        here = p_c[r]
        left = jnp.where(first, pltpu.roll(e_c[which], cols - 1 - 4 * r, axis=1), pltpu.roll(here, 1, axis=1))
        return p_t[r, 8 : deep + 8] - p_t[r, 7 : deep + 7] + p_r[r + 1] - p_r[r] + here - left

    p_r[0] = jnp.zeros((deep, cols), jnp.float32)

    def first_pass(r):
        store(r, unit(*slopes(r, 0)))

    def second_w(r):
        w[r, :deep] = divergence(r, 1) * inner_step + w[r, :deep]

    def second_pass(r):
        g_t, g_r, g_c = slopes(r, 2)
        store(r, unit(p_t[r, 8 : deep + 8] + g_t, p_r[r + 1] + g_r, p_c[r] + g_c))

    for r in range(wide):
        first_pass(r)
    for r in range(wide):
        second_w(r)
    w[wide, :deep] = w[wide - 1, :deep]
    for r in range(wide):
        second_pass(r)
    for r in range(rows):
        updated = v_ref[pl.ds(r, deep, stride=rows)] - theta * divergence(r + own, 3)
        p_c[r + own] = updated
        out_ref[pl.ds(r, frames, stride=rows)] = p_c[r + own, REACH : REACH + frames]


def on_chip(x):
    return pltpu.with_memory_space_constraint(x, pltpu.VMEM)


def on_chip_result(shape):
    return pltpu.VMEM(shape, jnp.float32)


def body(observed, kernel):
    frames, rows, cols = observed.shape
    taps = kernel.shape[0]
    half = taps // 2
    halo = 2 * half + REACH
    deep = -(-(frames + 2 * REACH) // 8) * 8
    count = lax.axis_size("tm")
    vmem = pl.BlockSpec(memory_space=pltpu.VMEM)
    f32 = jnp.float32

    mine = on_chip(observed.reshape(frames * rows, cols))
    far = pl.pallas_call(
        far_slice_kernel,
        out_shape=on_chip_result((halo * rows, cols)),
        in_specs=[pl.BlockSpec(memory_space=pl.ANY)],
        out_specs=vmem,
        scratch_shapes=[pltpu.SemaphoreType.DMA((COPIES,))],
        name="far_slice",
    )(observed.reshape(frames * rows, cols))
    near = pl.pallas_call(
        near_slice_kernel,
        out_shape=on_chip_result((halo * rows, cols)),
        in_specs=[vmem],
        out_specs=vmem,
        name="near_slice",
    )(mine)
    far = lax.ppermute(far, "tm", [(i, i + 1 if i % 2 else i - 1) for i in range(1, count - 1)])
    near = lax.ppermute(near, "tm", [(i, i ^ 1) for i in range(count)])
    near, far = on_chip(near), on_chip(far)

    def flat(count):
        return (count * rows, cols)

    shapes = [flat(n) for n in (taps, taps, half + 1, half + 1, frames - 2 * half - 2)]
    *taps_of, q_own = pl.pallas_call(
        own_kernel,
        out_shape=tuple(map(on_chip_result, shapes)),
        in_specs=[vmem] * 2,
        out_specs=(vmem,) * 5,
        name="own",
    )(mine, on_chip(kernel.reshape(taps * rows, cols)))
    taps_of, q_own = list(map(on_chip, taps_of)), on_chip(q_own)
    scratch = [pltpu.VMEM(flat(n), f32) for n in (2 * halo, deep + 2 * half, halo, halo)]
    q_far, v_far = pl.pallas_call(
        far_kernel,
        out_shape=(on_chip_result(flat(HALF)),) * 2,
        in_specs=[vmem] * 7,
        out_specs=(vmem,) * 2,
        scratch_shapes=scratch,
        name="far",
    )(far, mine, q_own, *taps_of)
    v, edge, message = pl.pallas_call(
        near_kernel,
        out_shape=tuple(map(on_chip_result, (flat(deep), (deep, cols), (4, REACH * (frames + 2 * REACH), cols)))),
        in_specs=[vmem] * 9,
        out_specs=(vmem,) * 3,
        scratch_shapes=scratch,
        name="near",
    )(near, mine, q_own, *taps_of, on_chip(q_far), on_chip(v_far))
    got = lax.all_to_all(message, ("row", "col"), 0, 0, tiled=True)

    wide = rows + REACH
    out = pl.pallas_call(
        tv_kernel,
        out_shape=jax.ShapeDtypeStruct((frames * rows, cols), f32),
        in_specs=[vmem] * 3,
        out_specs=vmem,
        scratch_shapes=[
            pltpu.VMEM((wide + 1, deep + 8, cols), f32),
            pltpu.VMEM((wide, deep + 8, cols), f32),
            pltpu.VMEM((wide + 1, deep, cols), f32),
            pltpu.VMEM((wide, deep, cols), f32),
            pltpu.VMEM((deep + 8, cols), f32),
            pltpu.VMEM((deep + 8, cols), f32),
            pltpu.VMEM((4, deep, cols), f32),
        ],
        name="tv",
    )(*map(on_chip, (v, edge, got)))
    return out.reshape(frames, rows, cols)


def solution(mesh):
    in_specs = (P("tm", "row", "col"), P(None, "row", "col"))
    out_specs = P("tm", "row", "col")
    return jax.shard_map(body, mesh=mesh, in_specs=in_specs, out_specs=out_specs, check_vma=False)
```
